32 devices in a mesh: dp: 4 (over y, x), expert: 8 (over z, core).
Axes of the slice: x: 2, y: 2, z: 4, core: 2. Of those that a mesh axis runs over, the one named last changes fastest.
Arguments:
- tokens: bfloat16 [8, 88, 4096], P('expert'), may hold values from -6 to 6
- routing: int32 [8, 88, 8], P('expert'), may hold values from 0 to 63, as said below
- combine: float32 [8, 88, 8], P('expert'), may hold values from 0.05 to 0.5
- w_gate: bfloat16 [64, 4096, 1536], P('expert', None, 'dp'), may hold values from -0.09375 to 0.09375
- w_up: bfloat16 [64, 4096, 1536], P('expert', None, 'dp'), may hold values from -0.09375 to 0.09375
- w_down: bfloat16 [64, 1536, 4096], P('expert', 'dp'), may hold values from -0.15625 to 0.15625
Outputs:
- mixed: bfloat16 [8, 88, 4096], P('expert', None, 'dp')
The draws below stay inside these ranges and needn't reach their ends.
Inputs may be any that keep to these rules, and one draw needn't show every extreme that they name: `routing`: each token names 8 different experts. In every group one expert, the same in all groups, is chosen by exactly 44 tokens; every other expert is chosen by 5 to 13 tokens of a group, and one of them, the same in all groups, by exactly 13 tokens of every group.
All inputs are finite; a program needn't handle non-finite values.
Results may differ from the reference program's by a relative error of at most 0.015.
Values may be sent and summed in bfloat16 or wider, within the bound.
No kernel may reach another device: no remote copies, remote signals or barrier semaphores. Data moves between devices by JAX's collectives and lax.ppermute only.
A program may use at most 192 MiB of HBM per device.

```python
import math
import jax
import jax.numpy as jnp
from jax import lax

D = 4096
FF = 1536
TOP = 8
EXPERTS = 64
GROUP_TOK = 88
GROUPS = 8
CAP = 13
LOW = 5
HOT_CAP = 44
N_DP = 4


def group_routes(key, hot_expert, full_cold):
    cold_count = EXPERTS - 1
    spare = CAP - LOW
    extra_total = GROUP_TOK * TOP - HOT_CAP - cold_count * LOW
    first_key, second_key, third_key = jax.random.split(key, 3)
    slot_total = cold_count * spare
    scores = jax.random.permutation(first_key, slot_total).astype(jnp.int32)
    slot_owner = jnp.arange(slot_total, dtype=jnp.int32) // spare
    scores = jnp.where(slot_owner == full_cold, scores - slot_total, scores)
    order = jnp.argsort(scores)
    slot_place = jnp.zeros((slot_total,), jnp.int32).at[order].set(jnp.arange(slot_total, dtype=jnp.int32))
    taken = (slot_place < extra_total).astype(jnp.int32)
    cold_counts = LOW + jnp.sum(taken.reshape(cold_count, spare), axis=1)
    expert_ids = jnp.arange(EXPERTS, dtype=jnp.int32)
    cold_index = jnp.clip(expert_ids - (expert_ids > hot_expert).astype(jnp.int32), 0, cold_count - 1)
    counts = jnp.where(expert_ids == hot_expert, HOT_CAP, cold_counts[cold_index])
    bounds = jnp.cumsum(counts).astype(jnp.int32)
    tickets = jnp.arange(GROUP_TOK * TOP, dtype=jnp.int32)
    expert_of = jnp.sum((tickets[:, None] >= bounds[None, :]).astype(jnp.int32), axis=1)
    table = expert_of.reshape(TOP, GROUP_TOK).T
    table = table[jax.random.permutation(second_key, GROUP_TOK)]
    shuffle = jax.random.randint(third_key, (GROUP_TOK, TOP), 0, 1 << 20) * TOP + jnp.arange(TOP, dtype=jnp.int32)[None, :]
    table = jnp.take_along_axis(table, jnp.argsort(shuffle, axis=1), axis=1)
    return table.astype(jnp.int32)


def draw_routing(key, part):
    hot_expert = jax.random.randint(jax.random.fold_in(key, 11), (), 0, EXPERTS)
    full_cold = jax.random.randint(jax.random.fold_in(key, 12), (), 0, EXPERTS - 1)
    group_keys = jax.random.split(jax.random.fold_in(key, 13), GROUPS)
    return jax.vmap(lambda one_key: group_routes(one_key, hot_expert, full_cold))(group_keys)


def block_levels(own_key, shape, shards, least, high):
    factor_of, own = 1.0, jax.random.fold_in(own_key, 6)
    for dim, blocks in shards:
        steps = jnp.exp(jax.random.uniform(jax.random.fold_in(own, dim), (blocks,), jnp.float32, least / len(shards), high / len(shards)))
        factor_of = factor_of * jnp.repeat(steps, shape[dim] // blocks).reshape([-1 if axis == dim else 1 for axis in range(len(shape))])
    return factor_of


def bell_draw(key, dims, spread, bound, shards=(), kind=jnp.bfloat16):
    drawn = jax.random.normal(key, dims, jnp.float32) * spread
    if len(shards) > 0:
        drawn = block_levels(key, dims, shards, -0.22, 0.18) * drawn
    return jnp.clip(drawn, min=-bound, max=bound).astype(kind)


def setup_inputs(seed: int = 0) -> dict:
    key_list = jax.random.split(jax.random.key(seed), 7)
    tokens = bell_draw(key_list[0], (GROUPS, GROUP_TOK, D), 1.0, 6.0, ((0, 8),))
    routing = draw_routing(jax.random.fold_in(key_list[6], 71), 0)
    combine = jnp.clip(jnp.exp(math.log(0.5) - 2.3025851 * jax.random.uniform(key_list[2], (GROUPS, GROUP_TOK, TOP), jnp.float32) ** block_levels(key_list[2], (GROUPS, GROUP_TOK, TOP), ((0, 8),), -0.2, 0.2)), 0.05, 0.5)
    w_gate = bell_draw(key_list[3], (EXPERTS, D, FF), D ** -0.5, 0.09375, ((0, 8), (2, 4)))
    w_up = bell_draw(key_list[4], (EXPERTS, D, FF), D ** -0.5, 0.09375, ((0, 8), (2, 4)))
    w_down = bell_draw(key_list[5], (EXPERTS, FF, D), FF ** -0.5, 0.15625, ((0, 8), (1, 4)))
    return {"tokens": tokens, "routing": routing, "combine": combine, "w_gate": w_gate, "w_up": w_up, "w_down": w_down}


def expert_rows(inputs, gate_mat, up_mat, down_mat, quarter):
    gate_val = jnp.dot(inputs, gate_mat, preferred_element_type=jnp.float32)
    up_val = jnp.dot(inputs, up_mat, preferred_element_type=jnp.float32)
    hidden = (jax.nn.silu(gate_val) * up_val).astype(jnp.bfloat16)
    total = jnp.zeros((inputs.shape[0], down_mat.shape[1]), jnp.float32)
    for part_idx in range(N_DP):
        lower = part_idx * quarter
        piece = jnp.dot(hidden[:, lower:lower + quarter], down_mat[lower:lower + quarter], preferred_element_type=jnp.float32)
        total = total + lax.optimization_barrier(piece.astype(jnp.bfloat16)).astype(jnp.float32)
    return total.astype(jnp.bfloat16)


def reference(tokens, routing, combine, w_gate, w_up, w_down):
    model_width = tokens.shape[2]
    token_rows = tokens.reshape(-1, model_width)
    num_tokens = token_rows.shape[0]
    top_k = routing.shape[2]
    pick_ids = routing.reshape(-1).astype(jnp.int32)
    assigns = pick_ids.shape[0]
    experts = w_gate.shape[0]
    quarter = w_gate.shape[2] // N_DP
    padded = jnp.concatenate([token_rows, jnp.zeros((1, model_width), token_rows.dtype)], axis=0)
    weight_flat = jnp.concatenate([combine.reshape(-1).astype(jnp.float32), jnp.zeros((1,), jnp.float32)], axis=0)
    counts = jnp.zeros((experts,), jnp.int32).at[pick_ids].add(jnp.ones((assigns,), jnp.int32))
    hot_expert = jnp.argmax(counts).astype(jnp.int32)
    positions = jnp.arange(assigns, dtype=jnp.int32)

    def one_expert(result, expert_id, capacity):
        member = (pick_ids == expert_id).astype(jnp.int32)
        slot_rank = (jnp.cumsum(member) - 1).astype(jnp.int32)
        where_to = jnp.where(member == 1, slot_rank, capacity).astype(jnp.int32)
        sources = jnp.full((capacity,), assigns, jnp.int32).at[where_to].set(positions, mode="drop")
        owner_tok = (sources // top_k).astype(jnp.int32)
        inputs = jnp.take(padded, owner_tok, axis=0)
        outputs = expert_rows(inputs, w_gate[expert_id], w_up[expert_id], w_down[expert_id], quarter)
        scaled = jnp.take(weight_flat, sources)[:, None] * outputs.astype(jnp.float32)
        return result.at[owner_tok].add(scaled)

    result = jnp.zeros((num_tokens + 1, model_width), jnp.float32)
    result = one_expert(result, hot_expert, GROUPS * HOT_CAP)

    def cold_step(carried, index):
        expert_id = (index + (index >= hot_expert).astype(jnp.int32)).astype(jnp.int32)
        return one_expert(carried, expert_id, GROUPS * CAP), index

    result = lax.scan(cold_step, result, jnp.arange(experts - 1, dtype=jnp.int32))[0]
    return result[:num_tokens].astype(jnp.bfloat16).reshape(tokens.shape)
```

```python
import functools

import jax
import jax.numpy as jnp
from jax import lax
from jax.experimental import pallas as pl
from jax.experimental.pallas import tpu as pltpu
from jax.sharding import PartitionSpec as P

CAP = 13
HOT_CAP = 44
AXES = ("dp", "expert")
BF16 = jnp.bfloat16
F32 = jnp.float32
VMEM_LIMIT = 56 * 1024 * 1024


def broadcast(block, axis, holder):
    block = jnp.where(lax.axis_index(axis) == holder, block, jnp.zeros_like(block))
    return lax.psum(block, axis)


def expert_partial(inputs, gate_mat, up_mat, down_mat):
    gate_val = jnp.dot(inputs, gate_mat, preferred_element_type=jnp.float32)
    up_val = jnp.dot(inputs, up_mat, preferred_element_type=jnp.float32)
    hidden = (jax.nn.silu(gate_val) * up_val).astype(jnp.bfloat16)
    return jnp.dot(hidden, down_mat, preferred_element_type=jnp.float32)


def dispatch_local(tokens, routing, combine, w_gate, w_up, w_down):
    group_rows = tokens[0]
    chosen = routing[0]
    mixing = combine[0]
    owners = lax.axis_size("expert")
    local_experts = w_gate.shape[0]
    experts = owners * local_experts
    group_tok, top_k = chosen.shape
    model_width = group_rows.shape[1]
    capacity = CAP
    hot_capacity = HOT_CAP
    pick_ids = chosen.reshape(-1)
    one_hot = (pick_ids[:, None] == jnp.arange(experts, dtype=jnp.int32)[None, :]).astype(jnp.int32)
    counts = jnp.sum(one_hot, axis=0)
    hot_expert = jnp.argmax(counts)
    slot_rank = jnp.sum((jnp.cumsum(one_hot, axis=0) - 1) * one_hot, axis=1)
    is_hot = pick_ids == hot_expert
    token_of = jnp.arange(pick_ids.shape[0], dtype=jnp.int32) // top_k
    cold_slot = jnp.where(is_hot, experts * capacity, pick_ids * capacity + slot_rank)
    slot_token = (
        jnp.full((experts * capacity,), group_tok, jnp.int32)
        .at[cold_slot]
        .set(token_of, mode="drop")
    )
    hot_slot = jnp.where(is_hot, slot_rank, hot_capacity)
    hot_token = (
        jnp.full((hot_capacity,), group_tok, jnp.int32).at[hot_slot].set(token_of, mode="drop")
    )
    padded = jnp.concatenate([group_rows, jnp.zeros((1, model_width), group_rows.dtype)], axis=0)
    outgoing = jnp.take(padded, slot_token, axis=0).reshape(
        owners, local_experts, capacity, model_width
    )
    local_pick = hot_expert % local_experts
    owner_index = hot_expert // local_experts
    own_gate = lax.dynamic_index_in_dim(w_gate, local_pick, 0, keepdims=False)
    own_up = lax.dynamic_index_in_dim(w_up, local_pick, 0, keepdims=False)
    own_down = lax.dynamic_index_in_dim(w_down, local_pick, 0, keepdims=False)
    hot_gate, hot_up, hot_down = (
        broadcast(own_gate, "expert", owner_index),
        broadcast(own_up, "expert", owner_index),
        broadcast(own_down, "expert", owner_index),
    )
    hot_partial = expert_partial(jnp.take(padded, hot_token, axis=0), hot_gate, hot_up, hot_down)
    received = lax.all_to_all(outgoing, "expert", split_axis=0, concat_axis=0, tiled=True)
    gate_val = jnp.einsum("senm,emf->senf", received, w_gate, preferred_element_type=jnp.float32)
    up_val = jnp.einsum("senm,emf->senf", received, w_up, preferred_element_type=jnp.float32)
    hidden = (jax.nn.silu(gate_val) * up_val).astype(jnp.bfloat16)
    partial_value = jnp.einsum("senf,efm->senm", hidden, w_down, preferred_element_type=jnp.float32)
    returned = lax.all_to_all(
        partial_value.astype(jnp.bfloat16), "expert", split_axis=0, concat_axis=0, tiled=True
    )
    flat_back = returned.reshape(experts * capacity, returned.shape[3])
    cold_sum, hot_sum = (
        lax.psum_scatter(flat_back, "dp", scatter_dimension=1, tiled=True).astype(jnp.float32),
        lax.psum_scatter(
            hot_partial.astype(jnp.bfloat16), "dp", scatter_dimension=1, tiled=True
        ).astype(jnp.float32),
    )
    cold_share = cold_sum.astype(jnp.bfloat16)
    hot_share = hot_sum.astype(jnp.bfloat16)
    out_table = jnp.concatenate([cold_share, hot_share], axis=0)
    target = jnp.where(
        is_hot, experts * capacity + slot_rank, pick_ids * capacity + slot_rank
    ).reshape(group_tok, top_k)
    combined = jnp.zeros((group_tok, out_table.shape[1]), jnp.float32)
    for column in range(top_k):
        picked = jnp.take(out_table, target[:, column], axis=0).astype(jnp.float32)
        combined = combined + mixing[:, column : column + 1] * picked
    return combined.astype(jnp.bfloat16)[None]


def gate_up_kernel(last, first, scal, onehot, hot_onehot, xa, xb, wg, wu, *rest):
    rest = list(rest)
    if not first:
        acc_in, hacc_in = rest.pop(0), rest.pop(0)
    if last:
        scale, hscale = rest.pop(0), rest.pop(0)
    out, hout, xg, xh = rest
    e = pl.program_id(0)
    half = xa.shape[0]
    hot = scal[1]

    def gather(table):
        return (
            jnp.dot(table[:, :half], xa[...], preferred_element_type=F32)
            + jnp.dot(table[:, half:], xb[...], preferred_element_type=F32)
        ).astype(BF16)

    @pl.when(e == 0)
    def _():
        xg[...] = gather(onehot[...]).reshape(xg.shape)

    def finish(g, u, scale_col):
        return (g / (1.0 + jnp.exp(-g)) * u * scale_col).astype(BF16)

    def work(x, prev, scale_col):
        f = wg.shape[2]
        g = jnp.dot(x, wg[0], preferred_element_type=F32)
        u = jnp.dot(x, wu[0], preferred_element_type=F32)
        if prev is not None:
            g = g + prev[:, :f]
            u = u + prev[:, f:]
        if last:
            return finish(g, u, scale_col)
        return jnp.concatenate([g, u], axis=1)

    out[0] = work(xg[e], None if first else acc_in[0], scale[0] if last else None)

    @pl.when(e == hot)
    def _():
        xh[...] = gather(hot_onehot[...])
        hout[...] = work(xh[...], None if first else hacc_in[...], hscale[...] if last else None)


def gate_up(quarter, hot, onehot, hot_onehot, xa, xb, w_gate, w_up, acc, scales):
    n, width, f = w_gate.shape
    part = xa.shape[1]
    rows = onehot.shape[0] // n
    hrows = hot_onehot.shape[0]
    first, last = acc is None, scales is not None
    scal = jnp.stack([quarter, hot]).astype(jnp.int32)

    def whole(a):
        return pl.BlockSpec(a.shape, lambda e, s: (0,) * a.ndim)

    def per_expert(*tail):
        return pl.BlockSpec((1,) + tail, lambda e, s: (e,) + (0,) * len(tail))

    w_spec = pl.BlockSpec((1, part, f), lambda e, s: (e, s[0], 0))
    operands = [onehot, hot_onehot, xa, xb, w_gate, w_up]
    specs = [whole(onehot), whole(hot_onehot), whole(xa), whole(xb), w_spec, w_spec]
    if not first:
        operands += list(acc)
        specs += [per_expert(rows, 2 * f), whole(acc[1])]
    if last:
        operands += list(scales)
        specs += [per_expert(rows, 1), whole(scales[1])]
    if last:
        outs = (jax.ShapeDtypeStruct((n, rows, f), BF16), jax.ShapeDtypeStruct((hrows, f), BF16))
    else:
        outs = (jax.ShapeDtypeStruct((n, rows, 2 * f), F32), jax.ShapeDtypeStruct((hrows, 2 * f), F32))
    return pl.pallas_call(
        functools.partial(gate_up_kernel, last, first),
        grid_spec=pltpu.PrefetchScalarGridSpec(
            num_scalar_prefetch=1,
            grid=(n,),
            in_specs=specs,
            out_specs=(per_expert(*outs[0].shape[1:]), pl.BlockSpec(outs[1].shape, lambda e, s: (0, 0))),
            scratch_shapes=[pltpu.VMEM((n, rows, part), BF16), pltpu.VMEM((hrows, part), BF16)],
        ),
        out_shape=outs,
        compiler_params=pltpu.CompilerParams(vmem_limit_bytes=VMEM_LIMIT),
        cost_estimate=pl.CostEstimate(
            flops=4 * n * rows * part * f + 4 * n * rows * xa.shape[0] * part,
            bytes_accessed=4 * n * part * f + 4 * xa.size,
            transcendentals=0,
        ),
        name="gate_up",
    )(scal, *operands)


def down_kernel(scal, spread, hot_spread, hidden, hhidden, wd, out_a, out_b, y, yh):
    e = pl.program_id(0)
    hot = scal[1]
    rows = hidden.shape[1]
    half = out_a.shape[0]
    at = pl.multiple_of(e * rows, 16)
    y[pl.ds(at, rows), :] = jnp.dot(hidden[0], wd[0], preferred_element_type=F32).astype(BF16)

    @pl.when(e == hot)
    def _():
        yh[...] = jnp.dot(hhidden[...], wd[0], preferred_element_type=F32).astype(BF16)

    last = e == pl.num_programs(0) - 1

    @pl.when(last & (hot < 0))
    def _():
        total = jnp.dot(spread[...], y[...], preferred_element_type=F32).astype(BF16)
        out_a[...] = total[:half]
        out_b[...] = total[half:]

    @pl.when(last & (hot >= 0))
    def _():
        total = jnp.dot(spread[...], y[...], preferred_element_type=F32)
        total = total + jnp.dot(hot_spread[...], yh[...], preferred_element_type=F32)
        total = total.astype(BF16)
        out_a[...] = total[:half]
        out_b[...] = total[half:]


def down(quarter, hot, spread, hot_spread, hidden, hhidden, w_down, part):
    n, f, width = w_down.shape
    tok, slots = spread.shape
    rows = hidden.shape[1]
    hrows = hhidden.shape[0]
    half = tok // 2
    scal = jnp.stack([quarter, hot]).astype(jnp.int32)

    def whole(a):
        return pl.BlockSpec(a.shape, lambda e, s: (0,) * a.ndim)

    out = jax.ShapeDtypeStruct((half, part), BF16)
    return pl.pallas_call(
        down_kernel,
        grid_spec=pltpu.PrefetchScalarGridSpec(
            num_scalar_prefetch=1,
            grid=(n,),
            in_specs=[
                whole(spread),
                whole(hot_spread),
                pl.BlockSpec((1, rows, f), lambda e, s: (e, 0, 0)),
                whole(hhidden),
                pl.BlockSpec((1, f, part), lambda e, s: (e, 0, s[0])),
            ],
            out_specs=(pl.BlockSpec(out.shape, lambda e, s: (0, 0)),) * 2,
            scratch_shapes=[pltpu.VMEM((n * rows, part), BF16), pltpu.VMEM((hrows, part), BF16)],
        ),
        out_shape=(out, out),
        compiler_params=pltpu.CompilerParams(vmem_limit_bytes=VMEM_LIMIT),
        cost_estimate=pl.CostEstimate(
            flops=2 * n * rows * part * f + 2 * n * rows * tok * part,
            bytes_accessed=2 * n * part * f + 4 * tok * part,
            transcendentals=0,
        ),
        name="down",
    )(scal, spread, hot_spread, hidden, hhidden, w_down)


def mover(n_dp, n_ex, step):
    pairs = []
    for d in range(n_dp):
        for e in range(n_ex):
            d2, z2, c2 = step(d, e // 2, e % 2)
            pairs.append((d * n_ex + e, d2 * n_ex + z2 * 2 + c2))
    return lambda x: lax.ppermute(x, AXES, pairs)


def gather_local(n_dp, n_ex, tokens, routing, combine, w_gate, w_up, w_down):
    lines = n_ex // 2
    rows = tokens[0]
    group_tok, width = rows.shape
    top_k = routing.shape[2]
    n = w_gate.shape[0]
    part = width // n_dp
    dp, me = lax.axis_index("dp"), lax.axis_index("expert")
    along = [mover(n_dp, n_ex, lambda d, z, c, s=s: (d, (z + s) % lines, c)) for s in range(lines)]
    across = [mover(n_dp, n_ex, lambda d, z, c, r=r: (d ^ r, z, c)) for r in range(n_dp)]
    swap = mover(n_dp, n_ex, lambda d, z, c: (d, z, 1 - c))

    info = jnp.concatenate([routing[0].astype(F32), combine[0]], axis=1).T
    column = jnp.concatenate([info] + [along[s](info) for s in range(1, lines)], axis=1)
    table = jnp.concatenate([column, swap(column)], axis=1)
    tok = table.shape[1]

    mine = [lax.dynamic_slice(rows, (0, (dp ^ r) * part), (group_tok, part)) for r in range(n_dp)]
    far = [along[s](mine[0]) for s in range(1, lines)]
    halves = []
    for r in range(n_dp):
        got = far if r == 0 else [across[r](piece) for piece in far]
        halves.append(jnp.concatenate([mine[r]] + got, axis=0))
    others = [swap(piece) for piece in halves]

    cold_rows = -(-CAP * n_ex // 16) * 16
    hot_rows = HOT_CAP * n_ex
    picks = table[:top_k].astype(jnp.int32)
    weights = table[top_k:]
    here = picks[None] == (me * n + jnp.arange(n, dtype=jnp.int32))[:, None, None]
    member = jnp.any(here, axis=1)
    weight = jnp.sum(jnp.where(here, weights[None], 0.0), axis=1)
    count = jnp.sum(member.astype(jnp.int32), axis=1)
    busiest = count > CAP * n_ex
    hot = jnp.where(jnp.any(busiest), jnp.argmax(busiest), -1).astype(jnp.int32)
    upto = (jnp.arange(tok)[:, None] <= jnp.arange(tok)[None, :]).astype(BF16)
    rank = jnp.dot(member.astype(BF16), upto, preferred_element_type=F32).astype(jnp.int32) - 1
    place = jnp.where(member & ~busiest[:, None], rank, -1)
    hot_place = jnp.max(jnp.where(member & busiest[:, None], rank, -1), axis=0)
    hot_weight = jnp.sum(jnp.where(busiest[:, None], weight, 0.0), axis=0)
    sit = place[:, None, :] == jnp.arange(cold_rows, dtype=jnp.int32)[None, :, None]
    hot_sit = hot_place[None, :] == jnp.arange(hot_rows, dtype=jnp.int32)[:, None]
    onehot = sit.astype(BF16).reshape(n * cold_rows, tok)
    hot_onehot = hot_sit.astype(BF16)
    scale = jnp.sum(jnp.where(sit, weight[:, None, :], 0.0), axis=2)[:, :, None]
    hot_scale = jnp.sum(jnp.where(hot_sit, hot_weight[None, :], 0.0), axis=1)[:, None]
    spread = onehot.T
    hot_spread = hot_onehot.T

    acc = None
    for r in range(n_dp):
        acc = gate_up(
            dp ^ r, hot, onehot, hot_onehot, halves[r], others[r], w_gate, w_up, acc,
            (scale, hot_scale) if r == n_dp - 1 else None,
        )
    hidden, hot_hidden = acc

    total = None
    for r in reversed(range(n_dp)):
        own, other = down(dp ^ r, hot, spread, hot_spread, hidden, hot_hidden, w_down, part)
        piece = (own.astype(F32) + swap(other).astype(F32)).astype(BF16)
        if r:
            piece = across[r](piece)
        piece = piece.astype(F32)
        total = piece if total is None else total + piece
    total = total.astype(BF16)
    out = total[:group_tok].astype(F32)
    for s in range(1, lines):
        out = out + along[lines - s](total[s * group_tok : (s + 1) * group_tok]).astype(F32)
    return out.astype(BF16)[None]


def solution(mesh):
    placed = (
        P("expert", None, None),
        P("expert", None, None),
        P("expert", None, None),
        P("expert", None, "dp"),
        P("expert", None, "dp"),
        P("expert", "dp", None),
    )
    n_dp, n_ex = mesh.shape["dp"], mesh.shape["expert"]
    short = n_ex <= 8 and n_ex % 2 == 0 and n_dp & (n_dp - 1) == 0
    local = functools.partial(gather_local, n_dp, n_ex) if short else dispatch_local
    return jax.shard_map(
        local, mesh=mesh, in_specs=placed, out_specs=P("expert", None, "dp"), check_vma=False
    )
```

```python
import functools

import jax
import jax.numpy as jnp
from jax import lax
from jax.experimental import pallas as pl
from jax.experimental.pallas import tpu as pltpu
from jax.sharding import PartitionSpec as P

CAP = 13
HOT_CAP = 44
AXES = ("dp", "expert")
BF16 = jnp.bfloat16
F32 = jnp.float32
VMEM_LIMIT = 60 * 1024 * 1024
COST = 0


def broadcast(block, axis, holder):
    block = jnp.where(lax.axis_index(axis) == holder, block, jnp.zeros_like(block))
    return lax.psum(block, axis)


def expert_partial(inputs, gate_mat, up_mat, down_mat):
    gate_val = jnp.dot(inputs, gate_mat, preferred_element_type=jnp.float32)
    up_val = jnp.dot(inputs, up_mat, preferred_element_type=jnp.float32)
    hidden = (jax.nn.silu(gate_val) * up_val).astype(jnp.bfloat16)
    return jnp.dot(hidden, down_mat, preferred_element_type=jnp.float32)


def dispatch_local(tokens, routing, combine, w_gate, w_up, w_down):
    group_rows = tokens[0]
    chosen = routing[0]
    mixing = combine[0]
    owners = lax.axis_size("expert")
    local_experts = w_gate.shape[0]
    experts = owners * local_experts
    group_tok, top_k = chosen.shape
    model_width = group_rows.shape[1]
    capacity = CAP
    hot_capacity = HOT_CAP
    pick_ids = chosen.reshape(-1)
    one_hot = (pick_ids[:, None] == jnp.arange(experts, dtype=jnp.int32)[None, :]).astype(jnp.int32)
    counts = jnp.sum(one_hot, axis=0)
    hot_expert = jnp.argmax(counts)
    slot_rank = jnp.sum((jnp.cumsum(one_hot, axis=0) - 1) * one_hot, axis=1)
    is_hot = pick_ids == hot_expert
    token_of = jnp.arange(pick_ids.shape[0], dtype=jnp.int32) // top_k
    cold_slot = jnp.where(is_hot, experts * capacity, pick_ids * capacity + slot_rank)
    slot_token = (
        jnp.full((experts * capacity,), group_tok, jnp.int32)
        .at[cold_slot]
        .set(token_of, mode="drop")
    )
    hot_slot = jnp.where(is_hot, slot_rank, hot_capacity)
    hot_token = (
        jnp.full((hot_capacity,), group_tok, jnp.int32).at[hot_slot].set(token_of, mode="drop")
    )
    padded = jnp.concatenate([group_rows, jnp.zeros((1, model_width), group_rows.dtype)], axis=0)
    outgoing = jnp.take(padded, slot_token, axis=0).reshape(
        owners, local_experts, capacity, model_width
    )
    local_pick = hot_expert % local_experts
    owner_index = hot_expert // local_experts
    own_gate = lax.dynamic_index_in_dim(w_gate, local_pick, 0, keepdims=False)
    own_up = lax.dynamic_index_in_dim(w_up, local_pick, 0, keepdims=False)
    own_down = lax.dynamic_index_in_dim(w_down, local_pick, 0, keepdims=False)
    hot_gate, hot_up, hot_down = (
        broadcast(own_gate, "expert", owner_index),
        broadcast(own_up, "expert", owner_index),
        broadcast(own_down, "expert", owner_index),
    )
    hot_partial = expert_partial(jnp.take(padded, hot_token, axis=0), hot_gate, hot_up, hot_down)
    received = lax.all_to_all(outgoing, "expert", split_axis=0, concat_axis=0, tiled=True)
    gate_val = jnp.einsum("senm,emf->senf", received, w_gate, preferred_element_type=jnp.float32)
    up_val = jnp.einsum("senm,emf->senf", received, w_up, preferred_element_type=jnp.float32)
    hidden = (jax.nn.silu(gate_val) * up_val).astype(jnp.bfloat16)
    partial_value = jnp.einsum("senf,efm->senm", hidden, w_down, preferred_element_type=jnp.float32)
    returned = lax.all_to_all(
        partial_value.astype(jnp.bfloat16), "expert", split_axis=0, concat_axis=0, tiled=True
    )
    flat_back = returned.reshape(experts * capacity, returned.shape[3])
    cold_sum, hot_sum = (
        lax.psum_scatter(flat_back, "dp", scatter_dimension=1, tiled=True).astype(jnp.float32),
        lax.psum_scatter(
            hot_partial.astype(jnp.bfloat16), "dp", scatter_dimension=1, tiled=True
        ).astype(jnp.float32),
    )
    cold_share = cold_sum.astype(jnp.bfloat16)
    hot_share = hot_sum.astype(jnp.bfloat16)
    out_table = jnp.concatenate([cold_share, hot_share], axis=0)
    target = jnp.where(
        is_hot, experts * capacity + slot_rank, pick_ids * capacity + slot_rank
    ).reshape(group_tok, top_k)
    combined = jnp.zeros((group_tok, out_table.shape[1]), jnp.float32)
    for column in range(top_k):
        picked = jnp.take(out_table, target[:, column], axis=0).astype(jnp.float32)
        combined = combined + mixing[:, column : column + 1] * picked
    return combined.astype(jnp.bfloat16)[None]


def scalars():
    return pl.BlockSpec(memory_space=pltpu.SMEM)


def outside():
    return pl.BlockSpec(memory_space=pltpu.HBM)


def inside():
    return pl.BlockSpec(memory_space=pltpu.VMEM)


def staged_kernel(body, n_scalars, n_in, n_out, *refs):
    given, rest = refs[:n_scalars], refs[n_scalars:]
    far_in, far_out, rest = rest[:n_in], rest[n_in : n_in + n_out], rest[n_in + n_out :]
    near_in, near_out, sem, rest = rest[-n_in - n_out - 1 : -n_out - 1], rest[-n_out - 1 : -1], rest[-1], rest[: -n_in - n_out - 1]
    loads = [pltpu.make_async_copy(s, d, sem.at[i]) for i, (s, d) in enumerate(zip(far_in, near_in))]
    for copy in loads:
        copy.start()
    for copy in loads:
        copy.wait()
    body(*given, *near_in, *near_out, *rest)
    stores = [pltpu.make_async_copy(s, d, sem.at[n_in + i]) for i, (s, d) in enumerate(zip(near_out, far_out))]
    for copy in stores:
        copy.start()
    for copy in stores:
        copy.wait()


def staged(body, given, inputs, outs, extra_outs=(), scratch=(), cost=1_000_000, name=None):
    near = [pltpu.VMEM(a.shape, a.dtype) for a in list(inputs) + list(outs)]
    return pl.pallas_call(
        functools.partial(staged_kernel, body, len(given), len(inputs), len(outs)),
        in_specs=[scalars()] * len(given) + [outside()] * len(inputs),
        out_specs=(outside(),) * len(outs) + (scalars(),) * len(extra_outs),
        out_shape=tuple(outs) + tuple(extra_outs),
        scratch_shapes=list(scratch) + near + [pltpu.SemaphoreType.DMA((len(near),))],
        compiler_params=pltpu.CompilerParams(vmem_limit_bytes=VMEM_LIMIT),
        cost_estimate=pl.CostEstimate(flops=0, bytes_accessed=cost, transcendentals=0),
        name=name,
    )(*given, *inputs)


def pack_kernel(first, *rest):
    pieces, (near, tail, table) = rest[:-3], rest[-3:]
    group_tok = first.shape[0]
    width = near.shape[1]
    table[len(pieces) * group_tok :, :] = first[:, width:]
    tail[...] = pieces[-1][:, :width]
    for i, piece in enumerate(pieces):
        near[i * group_tok : (i + 1) * group_tok, :] = piece[:, :width]
        table[i * group_tok : (i + 1) * group_tok, :] = piece[:, width:]


def pack(first, pieces, width):
    group_tok, lanes = first.shape
    outs = (
        jax.ShapeDtypeStruct((len(pieces) * group_tok, width), BF16),
        jax.ShapeDtypeStruct((group_tok, width), BF16),
        jax.ShapeDtypeStruct(((1 + len(pieces)) * group_tok, lanes - width), BF16),
    )
    return staged(pack_kernel, [], [first, *pieces], outs, name="pack")


def places_kernel(top_k, cap, base, own, other, onehot, hot_onehot, spread, hot_spread, scale, hscale, hot_out, stage):
    half = own.shape[0]
    tok = 2 * half
    n, rows = scale.shape[0], scale.shape[1]
    hrows = hot_onehot.shape[0]
    stage[0:half, :] = own[...].astype(F32)
    stage[half:tok, :] = other[...].astype(F32)
    table = stage[...].T
    picks = table[0:top_k].astype(jnp.int32) - base[0]
    weights = table[top_k : 2 * top_k] + table[2 * top_k : 3 * top_k] + table[3 * top_k : 4 * top_k]
    here = [picks == e for e in range(n)]
    member = jnp.concatenate([jnp.max(h.astype(F32), axis=0, keepdims=True) for h in here], axis=0)
    weight = jnp.concatenate([jnp.sum(jnp.where(h, weights, 0.0), axis=0, keepdims=True) for h in here], axis=0)
    busiest = jnp.sum(member, axis=1, keepdims=True) > cap
    upto = lax.broadcasted_iota(jnp.int32, (tok, tok), 0) <= lax.broadcasted_iota(jnp.int32, (tok, tok), 1)
    rank = jnp.dot(member.astype(BF16), upto.astype(F32).astype(BF16), preferred_element_type=F32) - 1.0
    place = jnp.where((member > 0.0) & (rank < rows), rank, -1.0)
    hot_place = jnp.max(jnp.where((member > 0.0) & busiest, rank - rows, -1.0), axis=0, keepdims=True)
    hot_weight = jnp.sum(jnp.where(busiest, weight, 0.0), axis=0, keepdims=True)
    number = lax.broadcasted_iota(jnp.int32, (n, 1), 0).astype(F32)
    hot_out[0] = jnp.max(jnp.where(busiest, number, -1.0)).astype(jnp.int32)
    slot = lax.broadcasted_iota(jnp.int32, (rows, tok), 0).astype(F32)
    for e in range(n):
        sit = slot == place[e : e + 1]
        onehot[e * rows : (e + 1) * rows, :] = sit.astype(F32).astype(BF16)
        scale[e] = jnp.sum(jnp.where(sit, weight[e : e + 1], 0.0), axis=1, keepdims=True)
    slot = lax.broadcasted_iota(jnp.int32, (hrows, tok), 0).astype(F32)
    sit = slot == hot_place
    hot_onehot[...] = sit.astype(F32).astype(BF16)
    hscale[...] = jnp.sum(jnp.where(sit, hot_weight, 0.0), axis=1, keepdims=True)
    spread[...] = onehot[...].T
    hot_spread[...] = hot_onehot[...].T


def places(base, own, other, n, groups, top_k):
    tok = 2 * own.shape[0]
    rows = -(-CAP * groups // 16) * 16
    hrows = -(-(HOT_CAP * groups - rows) // 16) * 16
    outs = (
        jax.ShapeDtypeStruct((n * rows, tok), BF16),
        jax.ShapeDtypeStruct((hrows, tok), BF16),
        jax.ShapeDtypeStruct((tok, n * rows), BF16),
        jax.ShapeDtypeStruct((tok, hrows), BF16),
        jax.ShapeDtypeStruct((n, rows, 1), F32),
        jax.ShapeDtypeStruct((hrows, 1), F32),
    )
    return staged(
        functools.partial(places_kernel, top_k, CAP * groups), [base], [own, other], outs,
        [jax.ShapeDtypeStruct((1,), jnp.int32)], [pltpu.VMEM((tok, own.shape[1]), F32)], 15_000_000, "places",
    )


def gate_up_kernel(counts, first, last, depth, quarter, busy, wg, wu, mine, theirs, *rest):
    nq = len(counts)
    rest = list(rest)

    def take(count):
        taken, rest[:count] = rest[:count], []
        return taken

    far = [take(2 * count) for count in counts]
    loaded = take(2 + (0 if first else 2) + (2 if last else 0))
    out, hout = take(2)
    near_v = [take(2 * count) for count in counts]
    loaded_v = take(len(loaded))
    onehot, hot_onehot = loaded_v[:2]
    prev, hprev = (None, None) if first else loaded_v[2:4]
    scale, hscale = loaded_v[-2:] if last else (None, None)
    total, htotal = (out, hout) if last else take(2)
    own, x, xg, xh, held, sem, load_sem, far_sem, own_sem, out_sem = rest
    n, _, f = wg.shape
    rows = xg.shape[1]
    group_tok, part = own.shape[2:]
    half = x.shape[0] // 2
    hot = busy[0]

    def start_of(i):
        return pl.multiple_of(quarter[i] * part, part)

    def copies(e, slot):
        return [
            pltpu.make_async_copy(
                w.at[e, pl.ds(start_of(i), part), :],
                held.at[slot, m, pl.ds(i * part, part), :],
                sem.at[slot, m, i],
            )
            for m, w in enumerate((wg, wu))
            for i in range(nq)
        ]

    loads = [pltpu.make_async_copy(s, d, load_sem.at[k]) for k, (s, d) in enumerate(zip(loaded, loaded_v))]
    pieces = []
    for i in range(nq):
        group = [
            pltpu.make_async_copy(w.at[:, pl.ds(start_of(i), part)], own.at[i, k], own_sem.at[i, k])
            for k, w in enumerate((mine, theirs))
        ]
        group += [pltpu.make_async_copy(s, d, far_sem.at[i, k]) for k, (s, d) in enumerate(zip(far[i], near_v[i]))]
        pieces.append(group)

    def start(copies):
        for copy in copies:
            copy.start()

    start(loads[:2] + pieces[0])
    ahead = [copies(e, e) for e in range(min(depth, n))]
    ahead = [sum(pieces[1:], [])] + ahead[:1] + [loads[2:]] + ahead[1:]
    for i in range(nq):
        lanes = slice(i * part, (i + 1) * part)
        for copy in (loads[:2] if i == 0 else []) + pieces[i]:
            copy.wait()
        for _ in range(2 if i < nq - 1 else len(ahead)):
            start(ahead.pop(0))
        for k, values in enumerate((near_v[i][: counts[i]], near_v[i][counts[i] :])):
            at = k * half
            for value in values + [own.at[i, k]]:
                x[at : at + value.shape[0]] = value[...]
                at += value.shape[0]
        picked = jnp.dot(onehot[...], x[...], preferred_element_type=F32).astype(BF16)
        xg[:, :, lanes] = picked.reshape(n, rows, part)

        @pl.when(hot >= 0)
        def _(lanes=lanes):
            xh[:, lanes] = jnp.dot(hot_onehot[...], x[...], preferred_element_type=F32).astype(BF16)

    for copy in loads[2:]:
        copy.wait()

    def work(rows_in, slot, at, base, dst, scale_col):
        low, high = at + (slice(None), slice(0, f)), at + (slice(None), slice(f, 2 * f))
        g = jnp.dot(rows_in, held[slot, 0], preferred_element_type=F32)
        u = jnp.dot(rows_in, held[slot, 1], preferred_element_type=F32)
        if base is not None:
            g = g + base[low]
            u = u + base[high]
        if last:
            dst[at] = (g / (1.0 + jnp.exp(-g)) * u * scale_col).astype(BF16)
        else:
            dst[low] = g
            dst[high] = u

    def store(e):
        return pltpu.make_async_copy(total.at[e], out.at[e], out_sem.at[e])

    @pl.loop(0, n)
    def _(e):
        slot = lax.rem(e, depth)
        for copy in copies(e, slot):
            copy.wait()

        work(xg[e], slot, (e,), prev, total, scale[e] if last else None)

        @pl.when(e == hot)
        def _():
            work(xh[...], slot, (), hprev, htotal, hscale[...] if last else None)

        @pl.when(e + depth < n)
        def _():
            for copy in copies(e + depth, slot):
                copy.start()

        if not last:
            store(e).start()

    if not last:
        tail = pltpu.make_async_copy(htotal, hout, out_sem.at[n])
        tail.start()
        for e in range(n):
            store(e).wait()
        tail.wait()


def gate_up(quarters, hot, onehot, hot_onehot, mine, theirs, got, w_gate, w_up, acc, scales):
    n, width, f = w_gate.shape
    tok = onehot.shape[1]
    part = got[0][0].shape[1]
    rows = onehot.shape[0] // n
    hrows = hot_onehot.shape[0]
    nq = len(got)
    first, last = acc is None, scales is not None
    depth = min(n, 4)
    loaded = [onehot, hot_onehot] + ([] if first else list(acc)) + list(scales or ())
    far = [piece for pieces in got for piece in pieces]
    operands = [jnp.stack(quarters).astype(jnp.int32), hot, w_gate, w_up, mine, theirs] + far + loaded
    specs = [scalars()] * 2 + [outside()] * (len(operands) - 2)
    if last:
        outs = (jax.ShapeDtypeStruct((n, rows, f), BF16), jax.ShapeDtypeStruct((hrows, f), BF16))
    else:
        outs = (jax.ShapeDtypeStruct((n, rows, 2 * f), F32), jax.ShapeDtypeStruct((hrows, 2 * f), F32))
    scratch = [] if last else [pltpu.VMEM(o.shape, o.dtype) for o in outs]
    return pl.pallas_call(
        functools.partial(gate_up_kernel, tuple(len(p) // 2 for p in got), first, last, depth),
        in_specs=specs,
        out_specs=(inside(), inside()) if last else (outside(), outside()),
        out_shape=outs,
        scratch_shapes=[pltpu.VMEM(a.shape, a.dtype) for a in far + loaded]
        + scratch
        + [
            pltpu.VMEM((nq, 2, mine.shape[0], part), BF16),
            pltpu.VMEM((tok, part), BF16),
            pltpu.VMEM((n, rows, nq * part), BF16),
            pltpu.VMEM((hrows, nq * part), BF16),
            pltpu.VMEM((depth, 2, nq * part, f), BF16),
            pltpu.SemaphoreType.DMA((depth, 2, nq)),
            pltpu.SemaphoreType.DMA((len(loaded),)),
            pltpu.SemaphoreType.DMA((nq, max(len(p) for p in got))),
            pltpu.SemaphoreType.DMA((nq, 2)),
            pltpu.SemaphoreType.DMA((n + 1,)),
        ],
        compiler_params=pltpu.CompilerParams(vmem_limit_bytes=VMEM_LIMIT),
        cost_estimate=pl.CostEstimate(
            flops=0, bytes_accessed=COST * nq * n * part * f * 4, transcendentals=0
        ),
        name="gate_up",
    )(*operands)


def down_kernel(nq, quarter, busy, spread_far, hot_far, hidden, hhidden, wd, out_a, out_b, *scratch):
    spread, hot_spread, y, yh, held, sem, load_sem = scratch
    n, rows, _ = hidden.shape
    half = out_a.shape[0]
    part = y.shape[1]
    hot = busy[0]

    def copy(i, e):
        column = pl.ds(pl.multiple_of(quarter[i] * part, part), part)
        return pltpu.make_async_copy(wd.at[e, :, column], held.at[i, e], sem.at[i, e])

    pairs = (spread_far, spread), (hot_far, hot_spread)
    loads = [pltpu.make_async_copy(s, d, load_sem.at[k]) for k, (s, d) in enumerate(pairs)]
    steps = [(i, e) for i in range(nq) for e in range(n)]
    window = 6
    for step in steps[:window]:
        copy(*step).start()

    for i in range(nq):
        lanes = slice(i * part, (i + 1) * part)
        for e in range(n):
            copy(i, e).wait()
            for step in steps[i * n + e + window : i * n + e + window + 1]:
                copy(*step).start()
            if i == 0 and e < 2:
                loads[e].start()
            y[e * rows : (e + 1) * rows, :] = jnp.dot(hidden[e], held[i, e], preferred_element_type=F32).astype(BF16)

        @pl.when(hot >= 0)
        def _():
            yh[...] = jnp.dot(hhidden[...], held[i, hot], preferred_element_type=F32).astype(BF16)

        if i == 0:
            for load in loads:
                load.wait()

        @pl.when(hot < 0)
        def _():
            value = jnp.dot(spread[...], y[...], preferred_element_type=F32).astype(BF16)
            out_a[:, lanes] = value[:half]
            out_b[:, lanes] = value[half:]

        @pl.when(hot >= 0)
        def _():
            value = jnp.dot(spread[...], y[...], preferred_element_type=F32)
            value = value + jnp.dot(hot_spread[...], yh[...], preferred_element_type=F32)
            value = value.astype(BF16)
            out_a[:, lanes] = value[:half]
            out_b[:, lanes] = value[half:]


def down(quarters, hot, spread, hot_spread, hidden, hhidden, w_down, part):
    n, f, width = w_down.shape
    tok, slots = spread.shape
    rows = hidden.shape[1]
    hrows = hhidden.shape[0]
    nq = len(quarters)
    out = jax.ShapeDtypeStruct((tok // 2, nq * part), BF16)
    return pl.pallas_call(
        functools.partial(down_kernel, nq),
        in_specs=[scalars()] * 2 + [outside()] * 2 + [inside()] * 2 + [outside()],
        out_specs=(inside(), inside()),
        out_shape=(out, out),
        scratch_shapes=[
            pltpu.VMEM(spread.shape, BF16),
            pltpu.VMEM(hot_spread.shape, BF16),
            pltpu.VMEM((n * rows, part), BF16),
            pltpu.VMEM((hrows, part), BF16),
            pltpu.VMEM((nq, n, f, part), BF16),
            pltpu.SemaphoreType.DMA((nq, n)),
            pltpu.SemaphoreType.DMA((2,)),
        ],
        compiler_params=pltpu.CompilerParams(vmem_limit_bytes=46 * 1024 * 1024),
        cost_estimate=pl.CostEstimate(
            flops=0, bytes_accessed=COST * 2 * nq * n * part * f * 2, transcendentals=0
        ),
        name="down",
    )(jnp.stack(quarters).astype(jnp.int32), hot, spread, hot_spread, hidden, hhidden, w_down)


def mover(n_dp, n_ex, step):
    pairs = []
    for d in range(n_dp):
        for e in range(n_ex):
            d2, z2, c2 = step(d, e // 2, e % 2)
            pairs.append((d * n_ex + e, d2 * n_ex + z2 * 2 + c2))
    return lambda x: lax.ppermute(x, AXES, pairs)


def after(*values):
    return lax.optimization_barrier(values)


def gather_local(n_dp, n_ex, tokens, routing, combine, w_gate, w_up, w_down):
    lines = n_ex // 2
    rows = tokens[0]
    group_tok, width = rows.shape
    top_k = routing.shape[2]
    n = w_gate.shape[0]
    part = width // n_dp
    cut = part // 2
    dp, me = lax.axis_index("dp"), lax.axis_index("expert")
    along = [mover(n_dp, n_ex, lambda d, z, c, s=s: (d, (z + s) % lines, c)) for s in range(lines)]
    across = [mover(n_dp, n_ex, lambda d, z, c, r=r: (d ^ r, z, c)) for r in range(n_dp)]
    swap = mover(n_dp, n_ex, lambda d, z, c: (d, z, 1 - c))
    order = [1, 3, 2]

    mine = [lax.dynamic_slice(rows, (0, (dp ^ r) * part), (group_tok, part)) for r in (0, 3)]
    left, info = combine[0], [routing[0].astype(BF16)]
    for _ in range(3):
        term = lax.reduce_precision(left, 8, 7)
        info.append(term.astype(BF16))
        left = left - term
    blank = jnp.zeros((group_tok, -4 * top_k % 128), BF16)
    first = jnp.concatenate([mine[0]] + info + [blank], axis=1)
    theirs = swap(rows)
    got = after(theirs, *[along[s](first) for s in order])
    theirs, got = got[0], got[1:]
    corner = after(mine[1], *got)[0]
    near, tail, table = pack(first, got, part)
    corner = [along[s](corner) for s in order[:2]] + [across[3](tail)]
    by_x, by_y = across[1](near), across[2](near)
    table_other, near_other = swap(table), swap(near)
    onehot, hot_onehot, spread, hot_spread, scale, hot_scale, hot = places(
        (me * n).astype(jnp.int32)[None], table, table_other, n, n_ex, top_k
    )
    acc = gate_up([dp], hot, onehot, hot_onehot, rows, theirs, [[near, near_other]], w_gate, w_up, None, None)
    acc, by_x, by_y, corner = after(acc, by_x, by_y, corner)
    got = [list(pieces) + [swap(piece) for piece in pieces] for pieces in ((by_x,), (by_y,), corner)]
    hidden, hot_hidden = gate_up(
        [dp ^ 1, dp ^ 2, dp ^ 3], hot, onehot, hot_onehot, rows, theirs, got, w_gate, w_up, acc, (scale, hot_scale)
    )

    def partial(group, hot):
        own, other = down([dp ^ r for r in group], hot, spread, hot_spread, hidden, hot_hidden, w_down, part)
        half = own.shape[0] // 2
        found = []
        for i in range(len(group)):
            lanes = slice(i * part, (i + 1) * part)
            theirs = [swap(other[:half, lanes]), swap(other[half:, lanes])]
            found.append(own[:, lanes].astype(F32) + jnp.concatenate(theirs, axis=0).astype(F32))
        return found

    (p3,) = partial((3,), hot)
    p3 = p3.astype(BF16)
    hot, p3 = after(hot, p3)
    corner = across[3](p3)
    p1, p2 = partial((1, 2), hot)
    p1, p2 = p1.astype(BF16), p2.astype(BF16)
    hot, p1, p2, corner = after(hot, p1, p2, corner)
    by_x, by_y = across[1](p1), across[2](p2)
    (p0,) = partial((0,), hot)
    total = p0 + corner.astype(F32) + by_x.astype(F32) + by_y.astype(F32)
    out = total[(lines - 1) * group_tok :]
    for i, s in enumerate(order):
        out = out + along[lines - s](total[i * group_tok : (i + 1) * group_tok].astype(BF16)).astype(F32)
    return out.astype(BF16)[None]


def solution(mesh):
    placed = (
        P("expert", None, None),
        P("expert", None, None),
        P("expert", None, None),
        P("expert", None, "dp"),
        P("expert", None, "dp"),
        P("expert", "dp", None),
    )
    n_dp, n_ex = mesh.shape["dp"], mesh.shape["expert"]
    local = functools.partial(gather_local, n_dp, n_ex) if (n_dp, n_ex) == (4, 8) else dispatch_local
    return jax.shard_map(
        local, mesh=mesh, in_specs=placed, out_specs=P("expert", None, "dp"), check_vma=False
    )
```

```python
import functools

import jax
import jax.numpy as jnp
from jax import lax
from jax.experimental import pallas as pl
from jax.experimental.pallas import tpu as pltpu
from jax.sharding import PartitionSpec as P

CAP = 13
HOT_CAP = 44
AXES = ("dp", "expert")
BF16 = jnp.bfloat16
F32 = jnp.float32
VMEM_LIMIT = 60 * 1024 * 1024
COST = 0


def broadcast(block, axis, holder):
    block = jnp.where(lax.axis_index(axis) == holder, block, jnp.zeros_like(block))
    return lax.psum(block, axis)


def expert_partial(inputs, gate_mat, up_mat, down_mat):
    gate_val = jnp.dot(inputs, gate_mat, preferred_element_type=jnp.float32)
    up_val = jnp.dot(inputs, up_mat, preferred_element_type=jnp.float32)
    hidden = (jax.nn.silu(gate_val) * up_val).astype(jnp.bfloat16)
    return jnp.dot(hidden, down_mat, preferred_element_type=jnp.float32)


def dispatch_local(tokens, routing, combine, w_gate, w_up, w_down):
    group_rows = tokens[0]
    chosen = routing[0]
    mixing = combine[0]
    owners = lax.axis_size("expert")
    local_experts = w_gate.shape[0]
    experts = owners * local_experts
    group_tok, top_k = chosen.shape
    model_width = group_rows.shape[1]
    capacity = CAP
    hot_capacity = HOT_CAP
    pick_ids = chosen.reshape(-1)
    one_hot = (pick_ids[:, None] == jnp.arange(experts, dtype=jnp.int32)[None, :]).astype(jnp.int32)
    counts = jnp.sum(one_hot, axis=0)
    hot_expert = jnp.argmax(counts)
    slot_rank = jnp.sum((jnp.cumsum(one_hot, axis=0) - 1) * one_hot, axis=1)
    is_hot = pick_ids == hot_expert
    token_of = jnp.arange(pick_ids.shape[0], dtype=jnp.int32) // top_k
    cold_slot = jnp.where(is_hot, experts * capacity, pick_ids * capacity + slot_rank)
    slot_token = (
        jnp.full((experts * capacity,), group_tok, jnp.int32)
        .at[cold_slot]
        .set(token_of, mode="drop")
    )
    hot_slot = jnp.where(is_hot, slot_rank, hot_capacity)
    hot_token = (
        jnp.full((hot_capacity,), group_tok, jnp.int32).at[hot_slot].set(token_of, mode="drop")
    )
    padded = jnp.concatenate([group_rows, jnp.zeros((1, model_width), group_rows.dtype)], axis=0)
    outgoing = jnp.take(padded, slot_token, axis=0).reshape(
        owners, local_experts, capacity, model_width
    )
    local_pick = hot_expert % local_experts
    owner_index = hot_expert // local_experts
    own_gate = lax.dynamic_index_in_dim(w_gate, local_pick, 0, keepdims=False)
    own_up = lax.dynamic_index_in_dim(w_up, local_pick, 0, keepdims=False)
    own_down = lax.dynamic_index_in_dim(w_down, local_pick, 0, keepdims=False)
    hot_gate, hot_up, hot_down = (
        broadcast(own_gate, "expert", owner_index),
        broadcast(own_up, "expert", owner_index),
        broadcast(own_down, "expert", owner_index),
    )
    hot_partial = expert_partial(jnp.take(padded, hot_token, axis=0), hot_gate, hot_up, hot_down)
    received = lax.all_to_all(outgoing, "expert", split_axis=0, concat_axis=0, tiled=True)
    gate_val = jnp.einsum("senm,emf->senf", received, w_gate, preferred_element_type=jnp.float32)
    up_val = jnp.einsum("senm,emf->senf", received, w_up, preferred_element_type=jnp.float32)
    hidden = (jax.nn.silu(gate_val) * up_val).astype(jnp.bfloat16)
    partial_value = jnp.einsum("senf,efm->senm", hidden, w_down, preferred_element_type=jnp.float32)
    returned = lax.all_to_all(
        partial_value.astype(jnp.bfloat16), "expert", split_axis=0, concat_axis=0, tiled=True
    )
    flat_back = returned.reshape(experts * capacity, returned.shape[3])
    cold_sum, hot_sum = (
        lax.psum_scatter(flat_back, "dp", scatter_dimension=1, tiled=True).astype(jnp.float32),
        lax.psum_scatter(
            hot_partial.astype(jnp.bfloat16), "dp", scatter_dimension=1, tiled=True
        ).astype(jnp.float32),
    )
    cold_share = cold_sum.astype(jnp.bfloat16)
    hot_share = hot_sum.astype(jnp.bfloat16)
    out_table = jnp.concatenate([cold_share, hot_share], axis=0)
    target = jnp.where(
        is_hot, experts * capacity + slot_rank, pick_ids * capacity + slot_rank
    ).reshape(group_tok, top_k)
    combined = jnp.zeros((group_tok, out_table.shape[1]), jnp.float32)
    for column in range(top_k):
        picked = jnp.take(out_table, target[:, column], axis=0).astype(jnp.float32)
        combined = combined + mixing[:, column : column + 1] * picked
    return combined.astype(jnp.bfloat16)[None]


def scalars():
    return pl.BlockSpec(memory_space=pltpu.SMEM)


def outside():
    return pl.BlockSpec(memory_space=pltpu.HBM)


def inside():
    return pl.BlockSpec(memory_space=pltpu.VMEM)


def staged_kernel(body, n_scalars, n_in, n_out, *refs):
    given, rest = refs[:n_scalars], refs[n_scalars:]
    far_in, far_out, rest = rest[:n_in], rest[n_in : n_in + n_out], rest[n_in + n_out :]
    near_in, near_out, sem, rest = rest[-n_in - n_out - 1 : -n_out - 1], rest[-n_out - 1 : -1], rest[-1], rest[: -n_in - n_out - 1]
    loads = [pltpu.make_async_copy(s, d, sem.at[i]) for i, (s, d) in enumerate(zip(far_in, near_in))]
    for copy in loads:
        copy.start()
    for copy in loads:
        copy.wait()
    body(*given, *near_in, *near_out, *rest)
    stores = [pltpu.make_async_copy(s, d, sem.at[n_in + i]) for i, (s, d) in enumerate(zip(near_out, far_out))]
    for copy in stores:
        copy.start()
    for copy in stores:
        copy.wait()


def staged(body, given, inputs, outs, extra_outs=(), scratch=(), cost=1_000_000, name=None):
    near = [pltpu.VMEM(a.shape, a.dtype) for a in list(inputs) + list(outs)]
    return pl.pallas_call(
        functools.partial(staged_kernel, body, len(given), len(inputs), len(outs)),
        in_specs=[scalars()] * len(given) + [outside()] * len(inputs),
        out_specs=(outside(),) * len(outs) + (scalars(),) * len(extra_outs),
        out_shape=tuple(outs) + tuple(extra_outs),
        scratch_shapes=list(scratch) + near + [pltpu.SemaphoreType.DMA((len(near),))],
        compiler_params=pltpu.CompilerParams(vmem_limit_bytes=VMEM_LIMIT),
        cost_estimate=pl.CostEstimate(flops=0, bytes_accessed=cost, transcendentals=0),
        name=name,
    )(*given, *inputs)


def pack_kernel(first, *rest):
    pieces, (near, tail, table) = rest[:-3], rest[-3:]
    group_tok = first.shape[0]
    width = near.shape[1]
    table[len(pieces) * group_tok :, :] = first[:, width:]
    tail[...] = pieces[-1][:, :width]
    for i, piece in enumerate(pieces):
        near[i * group_tok : (i + 1) * group_tok, :] = piece[:, :width]
        table[i * group_tok : (i + 1) * group_tok, :] = piece[:, width:]


def pack(first, pieces, width):
    group_tok, lanes = first.shape
    outs = (
        jax.ShapeDtypeStruct((len(pieces) * group_tok, width), BF16),
        jax.ShapeDtypeStruct((group_tok, width), BF16),
        jax.ShapeDtypeStruct(((1 + len(pieces)) * group_tok, lanes - width), BF16),
    )
    return staged(pack_kernel, [], [first, *pieces], outs, name="pack")


def places_kernel(top_k, cap, base, own, other, onehot, hot_onehot, spread, hot_spread, scale, hscale, hot_out, stage):
    half = own.shape[0]
    tok = 2 * half
    n, rows = scale.shape[0], scale.shape[1]
    hrows = hot_onehot.shape[0]
    stage[0:half, :] = own[...].astype(F32)
    stage[half:tok, :] = other[...].astype(F32)
    table = stage[...].T
    picks = table[0:top_k].astype(jnp.int32) - base[0]
    weights = table[top_k : 2 * top_k] + table[2 * top_k : 3 * top_k] + table[3 * top_k : 4 * top_k]
    here = [picks == e for e in range(n)]
    member = jnp.concatenate([jnp.max(h.astype(F32), axis=0, keepdims=True) for h in here], axis=0)
    weight = jnp.concatenate([jnp.sum(jnp.where(h, weights, 0.0), axis=0, keepdims=True) for h in here], axis=0)
    busiest = jnp.sum(member, axis=1, keepdims=True) > cap
    upto = lax.broadcasted_iota(jnp.int32, (tok, tok), 0) <= lax.broadcasted_iota(jnp.int32, (tok, tok), 1)
    rank = jnp.dot(member.astype(BF16), upto.astype(F32).astype(BF16), preferred_element_type=F32) - 1.0
    place = jnp.where((member > 0.0) & (rank < rows), rank, -1.0)
    hot_place = jnp.max(jnp.where((member > 0.0) & busiest, rank - rows, -1.0), axis=0, keepdims=True)
    hot_weight = jnp.sum(jnp.where(busiest, weight, 0.0), axis=0, keepdims=True)
    number = lax.broadcasted_iota(jnp.int32, (n, 1), 0).astype(F32)
    hot_out[0] = jnp.max(jnp.where(busiest, number, -1.0)).astype(jnp.int32)
    slot = lax.broadcasted_iota(jnp.int32, (rows, tok), 0).astype(F32)
    for e in range(n):
        sit = slot == place[e : e + 1]
        onehot[e * rows : (e + 1) * rows, :] = sit.astype(F32).astype(BF16)
        scale[e] = jnp.sum(jnp.where(sit, weight[e : e + 1], 0.0), axis=1, keepdims=True)
    slot = lax.broadcasted_iota(jnp.int32, (hrows, tok), 0).astype(F32)
    sit = slot == hot_place
    hot_onehot[...] = sit.astype(F32).astype(BF16)
    hscale[...] = jnp.sum(jnp.where(sit, hot_weight, 0.0), axis=1, keepdims=True)
    spread[...] = onehot[...].T
    hot_spread[...] = hot_onehot[...].T


def places(base, own, other, n, groups, top_k):
    tok = 2 * own.shape[0]
    rows = -(-CAP * groups // 16) * 16
    hrows = -(-(HOT_CAP * groups - rows) // 16) * 16
    outs = (
        jax.ShapeDtypeStruct((n * rows, tok), BF16),
        jax.ShapeDtypeStruct((hrows, tok), BF16),
        jax.ShapeDtypeStruct((tok, n * rows), BF16),
        jax.ShapeDtypeStruct((tok, hrows), BF16),
        jax.ShapeDtypeStruct((n, rows, 1), F32),
        jax.ShapeDtypeStruct((hrows, 1), F32),
    )
    return staged(
        functools.partial(places_kernel, top_k, CAP * groups), [base], [own, other], outs,
        [jax.ShapeDtypeStruct((1,), jnp.int32)], [pltpu.VMEM((tok, own.shape[1]), F32)], 15_000_000, "places",
    )


def gate_up_kernel(counts, first, last, depth, quarter, busy, wg, wu, mine, theirs, *rest):
    nq = len(counts)
    rest = list(rest)

    def take(count):
        taken, rest[:count] = rest[:count], []
        return taken

    if last:
        spread_far, hot_far, wd = take(3)
    far = [take(2 * count) for count in counts]
    loaded = take(2 + (0 if first else 2) + (2 if last else 0))
    out, hout = take(2)
    if last:
        own_sum, *other_sum = take(3)
    near_v = [take(2 * count) for count in counts]
    loaded_v = take(len(loaded))
    onehot, hot_onehot = loaded_v[:2]
    prev, hprev = (None, None) if first else loaded_v[2:4]
    scale, hscale = loaded_v[-2:] if last else (None, None)
    total, htotal = take(2)
    if last:
        spread, hot_spread, y, yh, held_d, down_sem, spread_sem = take(7)
    own, x, xg, xh, held, sem, load_sem, far_sem, own_sem, out_sem = rest
    n, _, f = wg.shape
    rows = xg.shape[1]
    group_tok, part = own.shape[2:]
    half = x.shape[0] // 2
    hot = busy[0]

    def start_of(i):
        return pl.multiple_of(quarter[i] * part, part)

    def copies(e, slot):
        return [
            pltpu.make_async_copy(
                w.at[e, pl.ds(start_of(i), part), :],
                held.at[slot, m, pl.ds(i * part, part), :],
                sem.at[slot, m, i],
            )
            for m, w in enumerate((wg, wu))
            for i in range(nq)
        ]

    loads = [pltpu.make_async_copy(s, d, load_sem.at[k]) for k, (s, d) in enumerate(zip(loaded, loaded_v))]
    pieces = []
    for i in range(nq):
        group = [
            pltpu.make_async_copy(w.at[:, pl.ds(start_of(i), part)], own.at[i, k], own_sem.at[i, k])
            for k, w in enumerate((mine, theirs))
        ]
        group += [pltpu.make_async_copy(s, d, far_sem.at[i, k]) for k, (s, d) in enumerate(zip(far[i], near_v[i]))]
        pieces.append(group)

    def start(copies):
        for copy in copies:
            copy.start()

    start(loads[:2] + pieces[0] + copies(0, 0))
    ahead = [copies(e, e) for e in range(1, min(depth, n))]
    ahead = [sum(pieces[1:], [])] + ahead[:1] + [loads[2:]] + ahead[1:]
    for i in range(nq):
        lanes = slice(i * part, (i + 1) * part)
        for copy in (loads[:2] if i == 0 else []) + pieces[i]:
            copy.wait()
        for _ in range(2 if i < nq - 1 else len(ahead)):
            start(ahead.pop(0))
        for k, values in enumerate((near_v[i][: counts[i]], near_v[i][counts[i] :])):
            at = k * half
            for value in values + [own.at[i, k]]:
                x[at : at + value.shape[0]] = value[...]
                at += value.shape[0]
        picked = jnp.dot(onehot[...], x[...], preferred_element_type=F32).astype(BF16)
        xg[:, :, lanes] = picked.reshape(n, rows, part)

        @pl.when(hot >= 0)
        def _(lanes=lanes):
            xh[:, lanes] = jnp.dot(hot_onehot[...], x[...], preferred_element_type=F32).astype(BF16)

    for copy in loads[2:]:
        copy.wait()

    def work(rows_in, slot, at, base, dst, scale_col):
        low, high = at + (slice(None), slice(0, f)), at + (slice(None), slice(f, 2 * f))
        g = jnp.dot(rows_in, held[slot, 0], preferred_element_type=F32)
        u = jnp.dot(rows_in, held[slot, 1], preferred_element_type=F32)
        if base is not None:
            g = g + base[low]
            u = u + base[high]
        if last:
            dst[at] = (g / (1.0 + jnp.exp(-g)) * u * scale_col).astype(BF16)
        else:
            dst[low] = g
            dst[high] = u

    def down_copy(e):
        return pltpu.make_async_copy(wd.at[e, :, pl.ds(start_of(nq - 1), part)], held_d.at[e], down_sem.at[e])

    def store(e):
        return pltpu.make_async_copy(total.at[e], out.at[e], out_sem.at[e])

    @pl.loop(0, n)
    def _(e):
        slot = lax.rem(e, depth)
        for copy in copies(e, slot):
            copy.wait()

        work(xg[e], slot, (e,), prev, total, scale[e] if last else None)

        @pl.when(e == hot)
        def _():
            work(xh[...], slot, (), hprev, htotal, hscale[...] if last else None)

        @pl.when(e + depth < n)
        def _():
            for copy in copies(e + depth, slot):
                copy.start()

        if last:

            @pl.when(e >= n - depth)
            def _():
                for i in range(2):
                    down_copy((e - (n - depth)) * 2 + i).start()

        store(e).start()

    tail = pltpu.make_async_copy(htotal, hout, out_sem.at[n])
    tail.start()
    if last:
        pairs = (spread_far, spread), (hot_far, hot_spread)
        spreads = [pltpu.make_async_copy(s, d, spread_sem.at[k]) for k, (s, d) in enumerate(pairs)]
        start(spreads)

        def ready():
            for copy in spreads:
                copy.wait()

        down_step(
            total, htotal, held_d, hot, spread, hot_spread, y, yh, lambda e: down_copy(e).wait(), ready,
            lambda value: put_sums(value, own_sum, *other_sum),
        )
    for e in range(n):
        store(e).wait()
    tail.wait()


def gate_up(quarters, hot, onehot, hot_onehot, mine, theirs, got, w_gate, w_up, acc, scales, spreads, w_down):
    n, width, f = w_gate.shape
    tok = onehot.shape[1]
    part = got[0][0].shape[1]
    rows = onehot.shape[0] // n
    hrows = hot_onehot.shape[0]
    nq = len(got)
    first, last = acc is None, scales is not None
    depth = min(n, 4)
    loaded = [onehot, hot_onehot] + ([] if first else list(acc)) + list(scales or ())
    far = [piece for pieces in got for piece in pieces]
    operands = [jnp.stack(quarters).astype(jnp.int32), hot, w_gate, w_up, mine, theirs]
    operands += ([*spreads, w_down] if last else []) + far + loaded
    specs = [scalars()] * 2 + [outside()] * (len(operands) - 2)
    if last:
        outs = (jax.ShapeDtypeStruct((n, rows, f), BF16), jax.ShapeDtypeStruct((hrows, f), BF16))
    else:
        outs = (jax.ShapeDtypeStruct((n, rows, 2 * f), F32), jax.ShapeDtypeStruct((hrows, 2 * f), F32))
    scratch = [pltpu.VMEM(o.shape, o.dtype) for o in outs]
    out_specs = (outside(),) * 2
    if last:
        outs += sums_of(tok, part)
        out_specs += (inside(),) * 3
        scratch += [pltpu.VMEM(a.shape, BF16) for a in spreads] + [
            pltpu.VMEM((n * rows, part), BF16),
            pltpu.VMEM((hrows, part), BF16),
            pltpu.VMEM((n, f, part), BF16),
            pltpu.SemaphoreType.DMA((n,)),
            pltpu.SemaphoreType.DMA((2,)),
        ]
    return pl.pallas_call(
        functools.partial(gate_up_kernel, tuple(len(p) // 2 for p in got), first, last, depth),
        in_specs=specs,
        out_specs=out_specs,
        out_shape=outs,
        scratch_shapes=[pltpu.VMEM(a.shape, a.dtype) for a in far + loaded]
        + scratch
        + [
            pltpu.VMEM((nq, 2, mine.shape[0], part), BF16),
            pltpu.VMEM((tok, part), BF16),
            pltpu.VMEM((n, rows, nq * part), BF16),
            pltpu.VMEM((hrows, nq * part), BF16),
            pltpu.VMEM((depth, 2, nq * part, f), BF16),
            pltpu.SemaphoreType.DMA((depth, 2, nq)),
            pltpu.SemaphoreType.DMA((len(loaded),)),
            pltpu.SemaphoreType.DMA((nq, max(len(p) for p in got))),
            pltpu.SemaphoreType.DMA((nq, 2)),
            pltpu.SemaphoreType.DMA((n + 1,)),
        ],
        compiler_params=pltpu.CompilerParams(vmem_limit_bytes=VMEM_LIMIT),
        cost_estimate=pl.CostEstimate(
            flops=0, bytes_accessed=COST * nq * n * part * f * 4, transcendentals=0
        ),
        name="gate_up",
    )(*operands)


def sums_of(tok, part):
    return tuple(jax.ShapeDtypeStruct((tok // count, part), BF16) for count in (2, 4, 4))


def put_sums(value, own, *other):
    half = own.shape[0]
    own[...] = value[:half]
    for i, piece in enumerate(other):
        at = half + i * piece.shape[0]
        piece[...] = value[at : at + piece.shape[0]]


def down_step(hidden, hhidden, held, hot, spread, hot_spread, y, yh, before, ready, put):
    n, rows, _ = hidden.shape
    @pl.loop(0, n)
    def _(e):
        before(e)
        at = pl.multiple_of(e * rows, 16)
        y[pl.ds(at, rows), :] = jnp.dot(hidden[e], held[e], preferred_element_type=F32).astype(BF16)

    @pl.when(hot >= 0)
    def _():
        yh[...] = jnp.dot(hhidden[...], held[hot], preferred_element_type=F32).astype(BF16)

    ready()

    @pl.when(hot < 0)
    def _():
        put(jnp.dot(spread[...], y[...], preferred_element_type=F32).astype(BF16))

    @pl.when(hot >= 0)
    def _():
        value = jnp.dot(spread[...], y[...], preferred_element_type=F32)
        put((value + jnp.dot(hot_spread[...], yh[...], preferred_element_type=F32)).astype(BF16))


def down_kernel(nq, quarter, busy, spread_far, hot_far, hidden_far, hhidden_far, wd, *rest):
    outs, scratch = rest[: 3 * nq], rest[3 * nq :]
    spread, hot_spread, hidden, hhidden, y, yh, total, held, sem, load_sem = scratch
    n, rows, _ = hidden.shape
    part = y.shape[1]
    hot = busy[0]

    def copy(i, e):
        column = pl.ds(pl.multiple_of(quarter[i] * part, part), part)
        return pltpu.make_async_copy(wd.at[e, :, column], held.at[i, e], sem.at[i, e])

    pairs = (hidden_far, hidden), (hhidden_far, hhidden), (spread_far, spread), (hot_far, hot_spread)
    loads = [pltpu.make_async_copy(s, d, load_sem.at[k]) for k, (s, d) in enumerate(pairs)]
    steps, window = nq * n, 6
    loads[0].start()
    for e in range(window):
        copy(0, e).start()
    for load in loads[1:]:
        load.start()
    loads[0].wait()

    @pl.loop(0, nq)
    def _(i):
        def before(e):
            copy(i, e).wait()
            ahead = i * n + e + window

            @pl.when(ahead < steps)
            def _():
                copy(lax.div(ahead, n), lax.rem(ahead, n)).start()

            @pl.when((i == 0) & (e == 0))
            def _():
                loads[1].wait()

        def ready():
            @pl.when(i == 0)
            def _():
                loads[2].wait()
                loads[3].wait()

        def put_this(value):
            total[...] = value
            for q in range(nq):

                @pl.when(i == q)
                def _(q=q):
                    put_sums(total, *outs[3 * q : 3 * q + 3])

        down_step(hidden, hhidden, held.at[i], hot, spread, hot_spread, y, yh, before, ready, put_this)


def down(quarters, hot, spread, hot_spread, hidden, hhidden, w_down, part):
    n, f, width = w_down.shape
    tok, slots = spread.shape
    rows = hidden.shape[1]
    hrows = hhidden.shape[0]
    nq = len(quarters)
    outs = sums_of(tok, part) * nq
    return pl.pallas_call(
        functools.partial(down_kernel, nq),
        in_specs=[scalars()] * 2 + [outside()] * 5,
        out_specs=(inside(),) * len(outs),
        out_shape=outs,
        scratch_shapes=[
            pltpu.VMEM(spread.shape, BF16),
            pltpu.VMEM(hot_spread.shape, BF16),
            pltpu.VMEM(hidden.shape, BF16),
            pltpu.VMEM(hhidden.shape, BF16),
            pltpu.VMEM((n * rows, part), BF16),
            pltpu.VMEM((hrows, part), BF16),
            pltpu.VMEM((tok, part), BF16),
            pltpu.VMEM((nq, n, f, part), BF16),
            pltpu.SemaphoreType.DMA((nq, n)),
            pltpu.SemaphoreType.DMA((4,)),
        ],
        compiler_params=pltpu.CompilerParams(vmem_limit_bytes=46 * 1024 * 1024),
        cost_estimate=pl.CostEstimate(
            flops=0, bytes_accessed=COST * 2 * nq * n * part * f * 2, transcendentals=0
        ),
        name="down",
    )(jnp.stack(quarters).astype(jnp.int32), hot, spread, hot_spread, hidden, hhidden, w_down)


def mover(n_dp, n_ex, step):
    pairs = []
    for d in range(n_dp):
        for e in range(n_ex):
            d2, z2, c2 = step(d, e // 2, e % 2)
            pairs.append((d * n_ex + e, d2 * n_ex + z2 * 2 + c2))
    return lambda x: lax.ppermute(x, AXES, pairs)


def after(*values):
    return lax.optimization_barrier(values)


def gather_local(n_dp, n_ex, tokens, routing, combine, w_gate, w_up, w_down):
    lines = n_ex // 2
    rows = tokens[0]
    group_tok, width = rows.shape
    top_k = routing.shape[2]
    n = w_gate.shape[0]
    part = width // n_dp
    cut = part // 2
    dp, me = lax.axis_index("dp"), lax.axis_index("expert")
    along = [mover(n_dp, n_ex, lambda d, z, c, s=s: (d, (z + s) % lines, c)) for s in range(lines)]
    across = [mover(n_dp, n_ex, lambda d, z, c, r=r: (d ^ r, z, c)) for r in range(n_dp)]
    swap = mover(n_dp, n_ex, lambda d, z, c: (d, z, 1 - c))
    order = [1, 3, 2]

    mine = [lax.dynamic_slice(rows, (0, (dp ^ r) * part), (group_tok, part)) for r in (0, 3)]
    left, info = combine[0], [routing[0].astype(BF16)]
    for _ in range(3):
        term = lax.reduce_precision(left, 8, 7)
        info.append(term.astype(BF16))
        left = left - term
    blank = jnp.zeros((group_tok, -4 * top_k % 128), BF16)
    first = jnp.concatenate([mine[0]] + info + [blank], axis=1)
    theirs = swap(rows)
    got = after(theirs, *[along[s](first) for s in order])
    theirs, got = got[0], got[1:]
    corner = after(mine[1], *got)[0]
    near, tail, table = pack(first, got, part)
    corner = [along[s](corner) for s in order[:2]] + [across[3](tail)]
    by_x, by_y = across[1](near), across[2](near)
    table_other, near_other = swap(table), swap(near)
    onehot, hot_onehot, spread, hot_spread, scale, hot_scale, hot = places(
        (me * n).astype(jnp.int32)[None], table, table_other, n, n_ex, top_k
    )
    acc = gate_up([dp], hot, onehot, hot_onehot, rows, theirs, [[near, near_other]], w_gate, w_up, None, None, None, None)
    acc, by_x, by_y, corner = after(acc, by_x, by_y, corner)
    got = [list(pieces) + [swap(piece) for piece in pieces] for pieces in ((by_x,), (by_y,), corner)]
    hidden, hot_hidden, *p3 = gate_up(
        [dp ^ 1, dp ^ 2, dp ^ 3], hot, onehot, hot_onehot, rows, theirs, got, w_gate, w_up, acc, (scale, hot_scale),
        (spread, hot_spread), w_down,
    )

    def whole_sum(own, *other):
        return own.astype(F32) + jnp.concatenate(other, axis=0).astype(F32)

    def swapped(found):
        return [piece if i % 3 == 0 else swap(piece) for i, piece in enumerate(found)]

    def partial(group, hot):
        return swapped(down([dp ^ r for r in group], hot, spread, hot_spread, hidden, hot_hidden, w_down, part))

    far_rows = (lines - 1) * group_tok
    p3 = whole_sum(*swapped(p3)).astype(BF16)
    hot, p3 = after(hot, p3)
    corner = across[3](p3)
    p12 = partial((1, 2), hot)
    p12[0], p12[3], corner = after(p12[0], p12[3], corner)
    p1, p2 = whole_sum(*p12[:3]).astype(BF16), whole_sum(*p12[3:]).astype(BF16)
    hot, p1, p2 = after(hot, p1, p2)
    by_x, by_y = across[1](p1[:far_rows]), across[2](p2[:far_rows])
    p0 = partial((0,), hot)
    p0[0], by_x, by_y = after(p0[0], by_x, by_y)
    end_x, end_y = across[1](p1[far_rows:]), across[2](p2[far_rows:])
    p0 = whole_sum(*p0) + corner.astype(F32)
    total = (p0[:far_rows] + by_x.astype(F32) + by_y.astype(F32)).astype(BF16)
    found = [along[lines - s](total[i * group_tok : (i + 1) * group_tok]) for i, s in enumerate(order)]
    out = p0[far_rows:] + end_x.astype(F32) + end_y.astype(F32)
    for piece in found:
        out = out + piece.astype(F32)
    return out.astype(BF16)[None]


def solution(mesh):
    placed = (
        P("expert", None, None),
        P("expert", None, None),
        P("expert", None, None),
        P("expert", None, "dp"),
        P("expert", None, "dp"),
        P("expert", "dp", None),
    )
    n_dp, n_ex = mesh.shape["dp"], mesh.shape["expert"]
    local = functools.partial(gather_local, n_dp, n_ex) if (n_dp, n_ex) == (4, 8) else dispatch_local
    return jax.shard_map(
        local, mesh=mesh, in_specs=placed, out_specs=P("expert", None, "dp"), check_vma=False
    )
```

```python
import functools

import jax
import jax.numpy as jnp
from jax import lax
from jax.experimental import pallas as pl
from jax.experimental.pallas import tpu as pltpu
from jax.sharding import PartitionSpec as P

CAP = 13
HOT_CAP = 44
AXES = ("dp", "expert")
BF16 = jnp.bfloat16
F32 = jnp.float32
VMEM_LIMIT = 60 * 1024 * 1024
COST = 0


def broadcast(block, axis, holder):
    block = jnp.where(lax.axis_index(axis) == holder, block, jnp.zeros_like(block))
    return lax.psum(block, axis)


def expert_partial(inputs, gate_mat, up_mat, down_mat):
    gate_val = jnp.dot(inputs, gate_mat, preferred_element_type=jnp.float32)
    up_val = jnp.dot(inputs, up_mat, preferred_element_type=jnp.float32)
    hidden = (jax.nn.silu(gate_val) * up_val).astype(jnp.bfloat16)
    return jnp.dot(hidden, down_mat, preferred_element_type=jnp.float32)


def dispatch_local(tokens, routing, combine, w_gate, w_up, w_down):
    group_rows = tokens[0]
    chosen = routing[0]
    mixing = combine[0]
    owners = lax.axis_size("expert")
    local_experts = w_gate.shape[0]
    experts = owners * local_experts
    group_tok, top_k = chosen.shape
    model_width = group_rows.shape[1]
    capacity = CAP
    hot_capacity = HOT_CAP
    pick_ids = chosen.reshape(-1)
    one_hot = (pick_ids[:, None] == jnp.arange(experts, dtype=jnp.int32)[None, :]).astype(jnp.int32)
    counts = jnp.sum(one_hot, axis=0)
    hot_expert = jnp.argmax(counts)
    slot_rank = jnp.sum((jnp.cumsum(one_hot, axis=0) - 1) * one_hot, axis=1)
    is_hot = pick_ids == hot_expert
    token_of = jnp.arange(pick_ids.shape[0], dtype=jnp.int32) // top_k
    cold_slot = jnp.where(is_hot, experts * capacity, pick_ids * capacity + slot_rank)
    slot_token = (
        jnp.full((experts * capacity,), group_tok, jnp.int32)
        .at[cold_slot]
        .set(token_of, mode="drop")
    )
    hot_slot = jnp.where(is_hot, slot_rank, hot_capacity)
    hot_token = (
        jnp.full((hot_capacity,), group_tok, jnp.int32).at[hot_slot].set(token_of, mode="drop")
    )
    padded = jnp.concatenate([group_rows, jnp.zeros((1, model_width), group_rows.dtype)], axis=0)
    outgoing = jnp.take(padded, slot_token, axis=0).reshape(
        owners, local_experts, capacity, model_width
    )
    local_pick = hot_expert % local_experts
    owner_index = hot_expert // local_experts
    own_gate = lax.dynamic_index_in_dim(w_gate, local_pick, 0, keepdims=False)
    own_up = lax.dynamic_index_in_dim(w_up, local_pick, 0, keepdims=False)
    own_down = lax.dynamic_index_in_dim(w_down, local_pick, 0, keepdims=False)
    hot_gate, hot_up, hot_down = (
        broadcast(own_gate, "expert", owner_index),
        broadcast(own_up, "expert", owner_index),
        broadcast(own_down, "expert", owner_index),
    )
    hot_partial = expert_partial(jnp.take(padded, hot_token, axis=0), hot_gate, hot_up, hot_down)
    received = lax.all_to_all(outgoing, "expert", split_axis=0, concat_axis=0, tiled=True)
    gate_val = jnp.einsum("senm,emf->senf", received, w_gate, preferred_element_type=jnp.float32)
    up_val = jnp.einsum("senm,emf->senf", received, w_up, preferred_element_type=jnp.float32)
    hidden = (jax.nn.silu(gate_val) * up_val).astype(jnp.bfloat16)
    partial_value = jnp.einsum("senf,efm->senm", hidden, w_down, preferred_element_type=jnp.float32)
    returned = lax.all_to_all(
        partial_value.astype(jnp.bfloat16), "expert", split_axis=0, concat_axis=0, tiled=True
    )
    flat_back = returned.reshape(experts * capacity, returned.shape[3])
    cold_sum, hot_sum = (
        lax.psum_scatter(flat_back, "dp", scatter_dimension=1, tiled=True).astype(jnp.float32),
        lax.psum_scatter(
            hot_partial.astype(jnp.bfloat16), "dp", scatter_dimension=1, tiled=True
        ).astype(jnp.float32),
    )
    cold_share = cold_sum.astype(jnp.bfloat16)
    hot_share = hot_sum.astype(jnp.bfloat16)
    out_table = jnp.concatenate([cold_share, hot_share], axis=0)
    target = jnp.where(
        is_hot, experts * capacity + slot_rank, pick_ids * capacity + slot_rank
    ).reshape(group_tok, top_k)
    combined = jnp.zeros((group_tok, out_table.shape[1]), jnp.float32)
    for column in range(top_k):
        picked = jnp.take(out_table, target[:, column], axis=0).astype(jnp.float32)
        combined = combined + mixing[:, column : column + 1] * picked
    return combined.astype(jnp.bfloat16)[None]


def scalars():
    return pl.BlockSpec(memory_space=pltpu.SMEM)


def outside():
    return pl.BlockSpec(memory_space=pltpu.HBM)


def inside():
    return pl.BlockSpec(memory_space=pltpu.VMEM)


def staged_kernel(body, n_scalars, n_in, n_out, *refs):
    given, rest = refs[:n_scalars], refs[n_scalars:]
    far_in, far_out, rest = rest[:n_in], rest[n_in : n_in + n_out], rest[n_in + n_out :]
    near_in, near_out, sem, rest = rest[-n_in - n_out - 1 : -n_out - 1], rest[-n_out - 1 : -1], rest[-1], rest[: -n_in - n_out - 1]
    loads = [pltpu.make_async_copy(s, d, sem.at[i]) for i, (s, d) in enumerate(zip(far_in, near_in))]
    for copy in loads:
        copy.start()
    for copy in loads:
        copy.wait()
    body(*given, *near_in, *near_out, *rest)
    stores = [pltpu.make_async_copy(s, d, sem.at[n_in + i]) for i, (s, d) in enumerate(zip(near_out, far_out))]
    for copy in stores:
        copy.start()
    for copy in stores:
        copy.wait()


def staged(body, given, inputs, outs, extra_outs=(), scratch=(), cost=1_000_000, name=None):
    near = [pltpu.VMEM(a.shape, a.dtype) for a in list(inputs) + list(outs)]
    return pl.pallas_call(
        functools.partial(staged_kernel, body, len(given), len(inputs), len(outs)),
        in_specs=[scalars()] * len(given) + [outside()] * len(inputs),
        out_specs=(outside(),) * len(outs) + (scalars(),) * len(extra_outs),
        out_shape=tuple(outs) + tuple(extra_outs),
        scratch_shapes=list(scratch) + near + [pltpu.SemaphoreType.DMA((len(near),))],
        compiler_params=pltpu.CompilerParams(vmem_limit_bytes=VMEM_LIMIT),
        cost_estimate=pl.CostEstimate(flops=0, bytes_accessed=cost, transcendentals=0),
        name=name,
    )(*given, *inputs)


def pack_kernel(first, *rest):
    pieces, (near, tail, table) = rest[:-3], rest[-3:]
    group_tok = first.shape[0]
    width = near.shape[1]
    table[len(pieces) * group_tok :, :] = first[:, width:]
    tail[...] = pieces[-1][:, :width]
    for i, piece in enumerate(pieces):
        near[i * group_tok : (i + 1) * group_tok, :] = piece[:, :width]
        table[i * group_tok : (i + 1) * group_tok, :] = piece[:, width:]


def pack(first, pieces, width):
    group_tok, lanes = first.shape
    outs = (
        jax.ShapeDtypeStruct((len(pieces) * group_tok, width), BF16),
        jax.ShapeDtypeStruct((group_tok, width), BF16),
        jax.ShapeDtypeStruct(((1 + len(pieces)) * group_tok, lanes - width), BF16),
    )
    return staged(pack_kernel, [], [first, *pieces], outs, name="pack")


def places_kernel(top_k, cap, base, own, other, onehot, hot_onehot, spread, hot_spread, scale, hscale, hot_out, stage):
    half = own.shape[0]
    tok = 2 * half
    n, rows = scale.shape[0], scale.shape[1]
    hrows = hot_onehot.shape[0]
    stage[0:half, :] = own[...].astype(F32)
    stage[half:tok, :] = other[...].astype(F32)
    table = stage[...].T
    picks = table[0:top_k].astype(jnp.int32) - base[0]
    weights = table[top_k : 2 * top_k] + table[2 * top_k : 3 * top_k] + table[3 * top_k : 4 * top_k]
    here = [picks == e for e in range(n)]
    member = jnp.concatenate([jnp.max(h.astype(F32), axis=0, keepdims=True) for h in here], axis=0)
    weight = jnp.concatenate([jnp.sum(jnp.where(h, weights, 0.0), axis=0, keepdims=True) for h in here], axis=0)
    busiest = jnp.sum(member, axis=1, keepdims=True) > cap
    upto = lax.broadcasted_iota(jnp.int32, (tok, tok), 0) <= lax.broadcasted_iota(jnp.int32, (tok, tok), 1)
    rank = jnp.dot(member.astype(BF16), upto.astype(F32).astype(BF16), preferred_element_type=F32) - 1.0
    place = jnp.where((member > 0.0) & (rank < rows), rank, -1.0)
    hot_place = jnp.max(jnp.where((member > 0.0) & busiest, rank - rows, -1.0), axis=0, keepdims=True)
    hot_weight = jnp.sum(jnp.where(busiest, weight, 0.0), axis=0, keepdims=True)
    number = lax.broadcasted_iota(jnp.int32, (n, 1), 0).astype(F32)
    hot_out[0] = jnp.max(jnp.where(busiest, number, -1.0)).astype(jnp.int32)
    slot = lax.broadcasted_iota(jnp.int32, (rows, tok), 0).astype(F32)
    for e in range(n):
        sit = slot == place[e : e + 1]
        onehot[e * rows : (e + 1) * rows, :] = sit.astype(F32).astype(BF16)
        scale[e] = jnp.sum(jnp.where(sit, weight[e : e + 1], 0.0), axis=1, keepdims=True)
    slot = lax.broadcasted_iota(jnp.int32, (hrows, tok), 0).astype(F32)
    sit = slot == hot_place
    hot_onehot[...] = sit.astype(F32).astype(BF16)
    hscale[...] = jnp.sum(jnp.where(sit, hot_weight, 0.0), axis=1, keepdims=True)
    spread[...] = onehot[...].T
    hot_spread[...] = hot_onehot[...].T


def places(base, own, other, n, groups, top_k):
    tok = 2 * own.shape[0]
    rows = -(-CAP * groups // 16) * 16
    hrows = -(-(HOT_CAP * groups - rows) // 16) * 16
    outs = (
        jax.ShapeDtypeStruct((n * rows, tok), BF16),
        jax.ShapeDtypeStruct((hrows, tok), BF16),
        jax.ShapeDtypeStruct((tok, n * rows), BF16),
        jax.ShapeDtypeStruct((tok, hrows), BF16),
        jax.ShapeDtypeStruct((n, rows, 1), F32),
        jax.ShapeDtypeStruct((hrows, 1), F32),
    )
    return staged(
        functools.partial(places_kernel, top_k, CAP * groups), [base], [own, other], outs,
        [jax.ShapeDtypeStruct((1,), jnp.int32)], [pltpu.VMEM((tok, own.shape[1]), F32)], 15_000_000, "places",
    )


def gate_up_kernel(counts, first, last, depth, quarter, busy, wg, wu, mine, theirs, *rest):
    nq = len(counts)
    rest = list(rest)

    def take(count):
        taken, rest[:count] = rest[:count], []
        return taken

    if last:
        spread_far, hot_far, wd = take(3)
    far = [take(2 * count) for count in counts]
    loaded = take(2 + (0 if first else 2) + (2 if last else 0))
    out, hout = take(2)
    if last:
        own_sum, *other_sum = take(3)
    near_v = [take(2 * count) for count in counts]
    loaded_v = take(len(loaded))
    onehot, hot_onehot = loaded_v[:2]
    prev, hprev = (None, None) if first else loaded_v[2:4]
    scale, hscale = loaded_v[-2:] if last else (None, None)
    total, htotal = take(2)
    if last:
        spread, hot_spread, y, yh, held_d, down_sem, spread_sem = take(7)
    own, x, xg, xh, held, sem, load_sem, far_sem, own_sem, out_sem = rest
    n, _, f = wg.shape
    rows = xg.shape[1]
    group_tok, part = own.shape[2:]
    half = x.shape[0] // 2
    hot = busy[0]

    def start_of(i):
        return pl.multiple_of(quarter[i] * part, part)

    def copies(e, slot):
        return [
            pltpu.make_async_copy(
                w.at[e, pl.ds(start_of(i), part), :],
                held.at[slot, m, pl.ds(i * part, part), :],
                sem.at[slot, m, i],
            )
            for m, w in enumerate((wg, wu))
            for i in range(nq)
        ]

    loads = [pltpu.make_async_copy(s, d, load_sem.at[k]) for k, (s, d) in enumerate(zip(loaded, loaded_v))]
    pieces = []
    for i in range(nq):
        group = [
            pltpu.make_async_copy(w.at[:, pl.ds(start_of(i), part)], own.at[i, k], own_sem.at[i, k])
            for k, w in enumerate((mine, theirs))
        ]
        group += [pltpu.make_async_copy(s, d, far_sem.at[i, k]) for k, (s, d) in enumerate(zip(far[i], near_v[i]))]
        pieces.append(group)

    def start(copies):
        for copy in copies:
            copy.start()

    start(loads[:2] + sum(pieces, []))
    ahead = [copies(e, e) for e in range(min(depth, n))]
    ahead = ahead[:2] + [loads[2:]] + ahead[2:]
    for i in range(nq):
        lanes = slice(i * part, (i + 1) * part)
        for copy in (loads[:2] if i == 0 else []) + pieces[i]:
            copy.wait()
        for _ in range(2 if i < nq - 1 else len(ahead)):
            start(ahead.pop(0))
        for k, values in enumerate((near_v[i][: counts[i]], near_v[i][counts[i] :])):
            at = k * half
            for value in values + [own.at[i, k]]:
                x[at : at + value.shape[0]] = value[...]
                at += value.shape[0]
        picked = jnp.dot(onehot[...], x[...], preferred_element_type=F32).astype(BF16)
        xg[:, :, lanes] = picked.reshape(n, rows, part)

        @pl.when(hot >= 0)
        def _(lanes=lanes):
            xh[:, lanes] = jnp.dot(hot_onehot[...], x[...], preferred_element_type=F32).astype(BF16)

    for copy in loads[2:]:
        copy.wait()

    def work(rows_in, slot, at, base, dst, scale_col):
        low, high = at + (slice(None), slice(0, f)), at + (slice(None), slice(f, 2 * f))
        g = jnp.dot(rows_in, held[slot, 0], preferred_element_type=F32)
        u = jnp.dot(rows_in, held[slot, 1], preferred_element_type=F32)
        if base is not None:
            g = g + base[low]
            u = u + base[high]
        if last:
            dst[at] = (g / (1.0 + jnp.exp(-g)) * u * scale_col).astype(BF16)
        else:
            dst[low] = g
            dst[high] = u

    def down_copy(e):
        return pltpu.make_async_copy(wd.at[e, :, pl.ds(start_of(nq - 1), part)], held_d.at[e], down_sem.at[e])

    def store(e):
        return pltpu.make_async_copy(total.at[e], out.at[e], out_sem.at[e])

    @pl.loop(0, n)
    def _(e):
        slot = lax.rem(e, depth)
        for copy in copies(e, slot):
            copy.wait()

        work(xg[e], slot, (e,), prev, total, scale[e] if last else None)

        @pl.when(e == hot)
        def _():
            work(xh[...], slot, (), hprev, htotal, hscale[...] if last else None)

        @pl.when(e + depth < n)
        def _():
            for copy in copies(e + depth, slot):
                copy.start()

        if last:

            @pl.when(e >= n - depth)
            def _():
                for i in range(2):
                    down_copy((e - (n - depth)) * 2 + i).start()

        store(e).start()

    tail = pltpu.make_async_copy(htotal, hout, out_sem.at[n])
    tail.start()
    if last:
        pairs = (spread_far, spread), (hot_far, hot_spread)
        spreads = [pltpu.make_async_copy(s, d, spread_sem.at[k]) for k, (s, d) in enumerate(pairs)]
        start(spreads)

        def ready():
            for copy in spreads:
                copy.wait()

        down_step(
            total, htotal, held_d, hot, spread, hot_spread, y, yh, lambda e: down_copy(e).wait(), ready,
            lambda value: put_sums(value, own_sum, *other_sum),
        )
    for e in range(n):
        store(e).wait()
    tail.wait()


def gate_up(quarters, hot, onehot, hot_onehot, mine, theirs, got, w_gate, w_up, acc, scales, spreads, w_down):
    n, width, f = w_gate.shape
    tok = onehot.shape[1]
    part = got[0][0].shape[1]
    rows = onehot.shape[0] // n
    hrows = hot_onehot.shape[0]
    nq = len(got)
    first, last = acc is None, scales is not None
    depth = min(n, 4)
    loaded = [onehot, hot_onehot] + ([] if first else list(acc)) + list(scales or ())
    far = [piece for pieces in got for piece in pieces]
    operands = [jnp.stack(quarters).astype(jnp.int32), hot, w_gate, w_up, mine, theirs]
    operands += ([*spreads, w_down] if last else []) + far + loaded
    specs = [scalars()] * 2 + [outside()] * (len(operands) - 2)
    if last:
        outs = (jax.ShapeDtypeStruct((n, rows, f), BF16), jax.ShapeDtypeStruct((hrows, f), BF16))
    else:
        outs = (jax.ShapeDtypeStruct((n, rows, 2 * f), F32), jax.ShapeDtypeStruct((hrows, 2 * f), F32))
    scratch = [pltpu.VMEM(o.shape, o.dtype) for o in outs]
    out_specs = (outside(),) * 2
    if last:
        outs += sums_of(tok, part)
        out_specs += (inside(),) * 3
        scratch += [pltpu.VMEM(a.shape, BF16) for a in spreads] + [
            pltpu.VMEM((n * rows, part), BF16),
            pltpu.VMEM((hrows, part), BF16),
            pltpu.VMEM((n, f, part), BF16),
            pltpu.SemaphoreType.DMA((n,)),
            pltpu.SemaphoreType.DMA((2,)),
        ]
    return pl.pallas_call(
        functools.partial(gate_up_kernel, tuple(len(p) // 2 for p in got), first, last, depth),
        in_specs=specs,
        out_specs=out_specs,
        out_shape=outs,
        scratch_shapes=[pltpu.VMEM(a.shape, a.dtype) for a in far + loaded]
        + scratch
        + [
            pltpu.VMEM((nq, 2, mine.shape[0], part), BF16),
            pltpu.VMEM((tok, part), BF16),
            pltpu.VMEM((n, rows, nq * part), BF16),
            pltpu.VMEM((hrows, nq * part), BF16),
            pltpu.VMEM((depth, 2, nq * part, f), BF16),
            pltpu.SemaphoreType.DMA((depth, 2, nq)),
            pltpu.SemaphoreType.DMA((len(loaded),)),
            pltpu.SemaphoreType.DMA((nq, max(len(p) for p in got))),
            pltpu.SemaphoreType.DMA((nq, 2)),
            pltpu.SemaphoreType.DMA((n + 1,)),
        ],
        compiler_params=pltpu.CompilerParams(vmem_limit_bytes=VMEM_LIMIT),
        cost_estimate=pl.CostEstimate(
            flops=0, bytes_accessed=COST * nq * n * part * f * 4, transcendentals=0
        ),
        name="gate_up",
    )(*operands)


def sums_of(tok, part):
    return tuple(jax.ShapeDtypeStruct((tok // count, part), BF16) for count in (2, 4, 4))


def put_sums(value, own, *other):
    half = own.shape[0]
    own[...] = value[:half]
    for i, piece in enumerate(other):
        at = half + i * piece.shape[0]
        piece[...] = value[at : at + piece.shape[0]]


def down_step(hidden, hhidden, held, hot, spread, hot_spread, y, yh, before, ready, put):
    n, rows, _ = hidden.shape
    @pl.loop(0, n)
    def _(e):
        before(e)
        at = pl.multiple_of(e * rows, 16)
        y[pl.ds(at, rows), :] = jnp.dot(hidden[e], held[e], preferred_element_type=F32).astype(BF16)

    @pl.when(hot >= 0)
    def _():
        yh[...] = jnp.dot(hhidden[...], held[hot], preferred_element_type=F32).astype(BF16)

    ready()

    @pl.when(hot < 0)
    def _():
        put(jnp.dot(spread[...], y[...], preferred_element_type=F32).astype(BF16))

    @pl.when(hot >= 0)
    def _():
        value = jnp.dot(spread[...], y[...], preferred_element_type=F32)
        put((value + jnp.dot(hot_spread[...], yh[...], preferred_element_type=F32)).astype(BF16))


def down_kernel(nq, quarter, busy, spread_far, hot_far, hidden_far, hhidden_far, wd, *rest):
    outs, scratch = rest[: 3 * nq], rest[3 * nq :]
    spread, hot_spread, hidden, hhidden, y, yh, total, held, sem, load_sem = scratch
    n, rows, _ = hidden.shape
    part = y.shape[1]
    hot = busy[0]

    def copy(i, e):
        column = pl.ds(pl.multiple_of(quarter[i] * part, part), part)
        return pltpu.make_async_copy(wd.at[e, :, column], held.at[i, e], sem.at[i, e])

    pairs = (hidden_far, hidden), (hhidden_far, hhidden), (spread_far, spread), (hot_far, hot_spread)
    loads = [pltpu.make_async_copy(s, d, load_sem.at[k]) for k, (s, d) in enumerate(pairs)]
    steps, window = nq * n, 6
    loads[0].start()
    for e in range(window):
        copy(0, e).start()
    for load in loads[1:]:
        load.start()
    loads[0].wait()

    @pl.loop(0, nq)
    def _(i):
        def before(e):
            copy(i, e).wait()
            ahead = i * n + e + window

            @pl.when(ahead < steps)
            def _():
                copy(lax.div(ahead, n), lax.rem(ahead, n)).start()

            @pl.when((i == 0) & (e == 0))
            def _():
                loads[1].wait()

        def ready():
            @pl.when(i == 0)
            def _():
                loads[2].wait()
                loads[3].wait()

        def put_this(value):
            total[...] = value
            for q in range(nq):

                @pl.when(i == q)
                def _(q=q):
                    put_sums(total, *outs[3 * q : 3 * q + 3])

        down_step(hidden, hhidden, held.at[i], hot, spread, hot_spread, y, yh, before, ready, put_this)


def down(quarters, hot, spread, hot_spread, hidden, hhidden, w_down, part):
    n, f, width = w_down.shape
    tok, slots = spread.shape
    rows = hidden.shape[1]
    hrows = hhidden.shape[0]
    nq = len(quarters)
    outs = sums_of(tok, part) * nq
    return pl.pallas_call(
        functools.partial(down_kernel, nq),
        in_specs=[scalars()] * 2 + [outside()] * 5,
        out_specs=(inside(),) * len(outs),
        out_shape=outs,
        scratch_shapes=[
            pltpu.VMEM(spread.shape, BF16),
            pltpu.VMEM(hot_spread.shape, BF16),
            pltpu.VMEM(hidden.shape, BF16),
            pltpu.VMEM(hhidden.shape, BF16),
            pltpu.VMEM((n * rows, part), BF16),
            pltpu.VMEM((hrows, part), BF16),
            pltpu.VMEM((tok, part), BF16),
            pltpu.VMEM((nq, n, f, part), BF16),
            pltpu.SemaphoreType.DMA((nq, n)),
            pltpu.SemaphoreType.DMA((4,)),
        ],
        compiler_params=pltpu.CompilerParams(vmem_limit_bytes=46 * 1024 * 1024),
        cost_estimate=pl.CostEstimate(
            flops=0, bytes_accessed=COST * 2 * nq * n * part * f * 2, transcendentals=0
        ),
        name="down",
    )(jnp.stack(quarters).astype(jnp.int32), hot, spread, hot_spread, hidden, hhidden, w_down)


def mover(n_dp, n_ex, step):
    pairs = []
    for d in range(n_dp):
        for e in range(n_ex):
            d2, z2, c2 = step(d, e // 2, e % 2)
            pairs.append((d * n_ex + e, d2 * n_ex + z2 * 2 + c2))
    return lambda x: lax.ppermute(x, AXES, pairs)


def after(*values):
    return lax.optimization_barrier(values)


def gather_local(n_dp, n_ex, tokens, routing, combine, w_gate, w_up, w_down):
    lines = n_ex // 2
    rows = tokens[0]
    group_tok, width = rows.shape
    top_k = routing.shape[2]
    n = w_gate.shape[0]
    part = width // n_dp
    cut = part // 2
    dp, me = lax.axis_index("dp"), lax.axis_index("expert")
    along = [mover(n_dp, n_ex, lambda d, z, c, s=s: (d, (z + s) % lines, c)) for s in range(lines)]
    across = [mover(n_dp, n_ex, lambda d, z, c, r=r: (d ^ r, z, c)) for r in range(n_dp)]
    swap = mover(n_dp, n_ex, lambda d, z, c: (d, z, 1 - c))
    order = [1, 3, 2]

    mine = [lax.dynamic_slice(rows, (0, (dp ^ r) * part), (group_tok, part)) for r in (0, 3)]
    left, info = combine[0], [routing[0].astype(BF16)]
    for _ in range(3):
        term = lax.reduce_precision(left, 8, 7)
        info.append(term.astype(BF16))
        left = left - term
    blank = jnp.zeros((group_tok, -4 * top_k % 128), BF16)
    first = jnp.concatenate([mine[0]] + info + [blank], axis=1)
    theirs = swap(rows)
    got = after(theirs, *[along[s](first) for s in order])
    theirs, got = got[0], got[1:]
    corner = after(mine[1], got[-1])[0]
    near, tail, table = pack(first, got, part)
    corner = [along[s](corner) for s in order[:2]] + [across[3](tail)]
    by_x, by_y = across[1](near), across[2](near)
    table_other, near_other = swap(table), swap(near)
    onehot, hot_onehot, spread, hot_spread, scale, hot_scale, hot = places(
        (me * n).astype(jnp.int32)[None], table, table_other, n, n_ex, top_k
    )
    acc = gate_up([dp], hot, onehot, hot_onehot, rows, theirs, [[near, near_other]], w_gate, w_up, None, None, None, None)
    acc, by_x, by_y, corner = after(acc, by_x, by_y, corner)
    got = [list(pieces) + [swap(piece) for piece in pieces] for pieces in ((by_x,), (by_y,), corner)]
    hidden, hot_hidden, *p3 = gate_up(
        [dp ^ 1, dp ^ 2, dp ^ 3], hot, onehot, hot_onehot, rows, theirs, got, w_gate, w_up, acc, (scale, hot_scale),
        (spread, hot_spread), w_down,
    )

    def whole_sum(own, *other):
        return own.astype(F32) + jnp.concatenate(other, axis=0).astype(F32)

    def swapped(found):
        return [piece if i % 3 == 0 else swap(piece) for i, piece in enumerate(found)]

    def partial(group, hot):
        return swapped(down([dp ^ r for r in group], hot, spread, hot_spread, hidden, hot_hidden, w_down, part))

    far_rows = (lines - 1) * group_tok
    p3 = whole_sum(*swapped(p3)).astype(BF16)
    hot, p3 = after(hot, p3)
    corner = across[3](p3)
    p12 = partial((1, 2), hot)
    p12[0], p12[3], corner = after(p12[0], p12[3], corner)
    p1, p2 = whole_sum(*p12[:3]).astype(BF16), whole_sum(*p12[3:]).astype(BF16)
    hot, p1, p2 = after(hot, p1, p2)
    by_x, by_y = across[1](p1[:far_rows]), across[2](p2[:far_rows])
    p0 = partial((0,), hot)
    p0[0], by_x, by_y = after(p0[0], by_x, by_y)
    end_x, end_y = across[1](p1[far_rows:]), across[2](p2[far_rows:])
    p0 = whole_sum(*p0) + corner.astype(F32)
    total = (p0[:far_rows] + by_x.astype(F32) + by_y.astype(F32)).astype(BF16)
    found = [along[lines - s](total[i * group_tok : (i + 1) * group_tok]) for i, s in enumerate(order)]
    out = p0[far_rows:] + end_x.astype(F32) + end_y.astype(F32)
    for piece in found:
        out = out + piece.astype(F32)
    return out.astype(BF16)[None]


def solution(mesh):
    placed = (
        P("expert", None, None),
        P("expert", None, None),
        P("expert", None, None),
        P("expert", None, "dp"),
        P("expert", None, "dp"),
        P("expert", "dp", None),
    )
    n_dp, n_ex = mesh.shape["dp"], mesh.shape["expert"]
    local = functools.partial(gather_local, n_dp, n_ex) if (n_dp, n_ex) == (4, 8) else dispatch_local
    return jax.shard_map(
        local, mesh=mesh, in_specs=placed, out_specs=P("expert", None, "dp"), check_vma=False
    )
```
